1024 devices in a mesh: group: 32 (over z), fsdp: 32 (over y, x, core).
Axes of the slice: x: 4, y: 4, z: 32, core: 2. Of those that a mesh axis runs over, the one named last changes fastest.
Arguments:
- grad_blocks: bfloat16 [256, 1024, 1024], P('group', 'fsdp')
- stale_roots: bfloat16 [512, 1024, 1024], P('group', 'fsdp'), as said below
- fresh_roots: bfloat16 [512, 1024, 1024], P('group', 'fsdp'), as said below
- owner_list: int32 [32, 16], replicated, may hold values from 0 to 31, as said below
- slot_list: int32 [32, 16], replicated, may hold values from 0 to 15, as said below
- refresh_flags: int32 [32, 16], replicated, may hold values from 0 to 1
Outputs:
- updates: bfloat16 [256, 1024, 1024], P('group', 'fsdp')
The draws below stay inside these ranges and needn't reach their ends.
Inputs may be any that keep to these rules, and one draw needn't show every extreme that they name: `stale_roots`: every block is symmetric. `fresh_roots`: every block is symmetric. `owner_list`: within one row the 16 owners are distinct. `slot_list`: two flagged entries with the same owner have different slots; the flagged entries of some owner use all 16 of its slots.
All inputs are finite; a program needn't handle non-finite values.
Results may differ from the reference program's by a relative error of at most 0.0049.
Values may be sent and summed in bfloat16 or wider, within the bound.
A program may use at most 32 MiB of HBM per device.

```python
import math
import jax
import jax.numpy as jnp
from jax import lax

BS = 1024
ROOTS = 16
TOTAL_BLOCKS = 256
TOTAL_ROOTS = 512
N_GROUP = 32


def assignment(key):
    key_start, key_label, key_rank, key_count, key_busy = jax.random.split(key, 5)
    start_row = jax.random.permutation(key_start, N_GROUP)
    labels = jax.random.permutation(key_label, N_GROUP)
    latin_index = (start_row[:, None] + jnp.arange(ROOTS)[None, :]) % N_GROUP
    owner_table = labels[latin_index]
    rank_keys = jax.random.split(key_rank, N_GROUP)
    rank_table = jax.vmap(lambda sub_key: jax.random.permutation(sub_key, ROOTS))(rank_keys)
    counts = jax.random.randint(key_count, (N_GROUP,), 0, ROOTS + 1)
    busiest = jax.random.randint(key_busy, (), 0, N_GROUP)
    counts = jnp.where(jnp.arange(N_GROUP) == busiest, ROOTS, counts)
    slot_table = rank_table[owner_table, jnp.arange(ROOTS)[None, :]]
    flag_table = (slot_table < counts[owner_table]).astype(jnp.int32)
    return (owner_table.astype(jnp.int32), slot_table.astype(jnp.int32), flag_table)


def draw_owner_list(key, part):
    return assignment(key)[0]


def draw_slot_list(key, part):
    return assignment(key)[1]


def draw_refresh_flags(key, part):
    return assignment(key)[2]


def symmetric_roots(key, count):
    key_noise, key_diagonal = jax.random.split(key)
    sample_noise = jax.random.normal(key_noise, (count, BS, BS), jnp.float32)
    off_diagonal = (sample_noise + jnp.swapaxes(sample_noise, 1, 2)) * (0.5 / math.sqrt(2.0 * BS))
    diagonal = jax.random.uniform(key_diagonal, (count, BS, 1), jnp.float32, 1.5, 3.0)
    on_diagonal = jnp.arange(BS)[:, None] == jnp.arange(BS)[None, :]
    return jnp.where(on_diagonal[None], diagonal, off_diagonal).astype(jnp.bfloat16)


def draw_stale_roots(key, part):
    key = jax.random.fold_in(key, 21)
    return symmetric_roots(key, TOTAL_ROOTS)


def draw_fresh_roots(key, part):
    key = jax.random.fold_in(key, 37)
    return symmetric_roots(key, TOTAL_ROOTS)


def draw_grad_blocks(key, part):
    key = jax.random.fold_in(key, 11)
    key_noise, key_row, key_column = jax.random.split(key, 3)
    array_shape = (TOTAL_BLOCKS, BS, BS)
    row_rise = 3.0 ** (jnp.arange(BS, dtype=jnp.float32)[None, :, None] / BS)
    row_scale = jnp.exp(jax.random.uniform(key_row, (TOTAL_BLOCKS, BS, 1), jnp.float32) * math.log(10.0))
    column_scale = jnp.exp(jax.random.uniform(key_column, (TOTAL_BLOCKS, 1, BS), jnp.float32) * math.log(10.0))
    random_part = jax.random.normal(key_noise, array_shape, jnp.float32)
    return (0.05 * random_part * row_rise * row_scale * column_scale).astype(jnp.bfloat16)


def setup_inputs(seed: int = 0) -> dict:
    key_list = jax.random.split(jax.random.key(seed), 7)
    grad_blocks = draw_grad_blocks(jax.random.fold_in(key_list[6], 71), 0)
    stale_roots = draw_stale_roots(jax.random.fold_in(key_list[6], 71), 0)
    fresh_roots = draw_fresh_roots(jax.random.fold_in(key_list[6], 71), 0)
    owner_list = draw_owner_list(jax.random.fold_in(key_list[6], 71), 0)
    slot_list = draw_slot_list(jax.random.fold_in(key_list[6], 71), 0)
    refresh_flags = draw_refresh_flags(jax.random.fold_in(key_list[6], 71), 0)
    return {"grad_blocks": grad_blocks, "stale_roots": stale_roots, "fresh_roots": fresh_roots, "owner_list": owner_list, "slot_list": slot_list, "refresh_flags": refresh_flags}


epsilon = 1e-06

def reference(grad_blocks, stale_roots, fresh_roots, owner_list, slot_list, refresh_flags):
    root_count = owner_list.shape[1]
    block_count = root_count // 2
    fresh_index = (owner_list * root_count + slot_list).astype(jnp.int32)

    def select_root(group_index, root_number):
        fresh_root = fresh_roots[fresh_index[group_index, root_number]]
        stale_root = stale_roots[group_index * root_count + root_number]
        return jnp.where(refresh_flags[group_index, root_number] == 1, fresh_root, stale_root)

    def one_block(block_number):
        group_index = block_number // block_count
        block_index = block_number % block_count
        left_root = select_root(group_index, 2 * block_index)
        right_root = select_root(group_index, 2 * block_index + 1)
        grad_block = grad_blocks[block_number]
        left_product = jnp.dot(left_root, grad_block, preferred_element_type=jnp.float32).astype(jnp.bfloat16)
        product = jnp.dot(left_product, right_root, preferred_element_type=jnp.float32)
        grad_square = jnp.sum(jnp.square(grad_block.astype(jnp.float32)))
        update_square = jnp.sum(product * product)
        graft_ratio = jnp.sqrt(grad_square) * lax.rsqrt(update_square + epsilon)
        return (graft_ratio * product).astype(jnp.bfloat16)
    return lax.map(one_block, jnp.arange(grad_blocks.shape[0], dtype=jnp.int32))
```

```python
import functools

import jax
import jax.numpy as jnp
from jax import lax
from jax.experimental import pallas as pl
from jax.experimental.pallas import tpu as pltpu
from jax.sharding import PartitionSpec as P

epsilon = 1e-06
MESH = pl.DeviceIdType.MESH
GROUPS = 32
SHARDS = 32
ROOTS = 16
BLOCKS = 8
ROWS = 32
WIDTH = 1024
HALF = 512
TILE = 128
SUPER = 8
BAND = 640
REST = 384
REACH = 16
HOPS = 18
TRAINS = 4
STEPS = HOPS * TRAINS
DIST_ROWS = 2 * STEPS
OK_ROW = DIST_ROWS + 2 * REACH
TABLE_ROWS = OK_ROW + 8


def tile_return(
    scaled, exchanged_fn, shard_count, shard_pos, part_index, blocks, row_count, half_width
):
    row_half = part_index // 2
    group_span = shard_count // 2
    keep_half = (jnp.arange(2) == row_half)[:, None, None, None]
    outgoing_update = jnp.where(
        keep_half, scaled.reshape(1, group_span, row_count, half_width), jnp.bfloat16(0.0)
    )
    outgoing_update = outgoing_update.reshape(shard_count, row_count, half_width)
    returned = exchanged_fn(outgoing_update)
    returned = returned.reshape(blocks, 2, 2, row_count, half_width)
    chosen = jnp.take(returned, shard_pos // group_span, axis=1)
    return chosen.transpose(0, 2, 1, 3).reshape(blocks, row_count, 2 * half_width)


def whole_exchange(grad_blocks, stale_roots, fresh_roots, owner_list, slot_list, refresh_flags):
    group_count = lax.axis_size("group")
    shard_count = lax.axis_size("fsdp")
    group_pos = lax.axis_index("group")
    shard_pos = lax.axis_index("fsdp")
    blocks, row_count, block_width = grad_blocks.shape
    roots_held = stale_roots.shape[0]
    half_width = block_width // 2
    flagged = refresh_flags == 1
    owned_here = jnp.logical_and(owner_list == group_pos, flagged)
    picked = jnp.sum(jnp.where(owned_here, slot_list, 0), axis=1)
    holding = jnp.any(owned_here, axis=1)
    selector = jnp.logical_and(
        picked[:, None] == jnp.arange(roots_held)[None, :], holding[:, None]
    ).astype(jnp.bfloat16)
    outgoing = jnp.einsum(
        "ts,sxw->txw", selector, fresh_roots, preferred_element_type=jnp.float32
    ).astype(jnp.bfloat16)
    arrived = lax.all_to_all(outgoing, "group", split_axis=0, concat_axis=0, tiled=True)
    own_owner = owner_list[group_pos]
    own_flag = flagged[group_pos]
    chooser = (own_owner[:, None] == jnp.arange(group_count)[None, :]).astype(jnp.bfloat16)
    delivered = jnp.einsum(
        "rt,txw->rxw", chooser, arrived, preferred_element_type=jnp.float32
    ).astype(jnp.bfloat16)
    current = jnp.where(own_flag[:, None, None], delivered, stale_roots)
    grad_square = jnp.sum(jnp.square(grad_blocks.astype(jnp.float32)), axis=(1, 2))
    spread = shard_count // blocks
    block_pos = shard_pos // spread
    part_index = shard_pos % spread
    left_roots = current[0::2]
    right_roots = current[1::2]
    contract_rows = (((0,), (0,)), ((), ()))
    tile_shape = (blocks, 2, 2, row_count, half_width)
    whole_grad = lax.all_to_all(
        jnp.repeat(grad_blocks, spread, axis=0), "fsdp", split_axis=0, concat_axis=1, tiled=True
    ).reshape(block_width, block_width)
    left_half = left_roots.reshape(blocks, row_count, 2, half_width).transpose(0, 2, 1, 3)
    right_half = right_roots.reshape(blocks, row_count, 2, half_width).transpose(0, 2, 1, 3)
    pieces = jnp.concatenate(
        [
            jnp.broadcast_to(left_half[:, :, None], tile_shape),
            jnp.broadcast_to(right_half[:, None], tile_shape),
        ],
        axis=4,
    ).reshape(shard_count, row_count, block_width)
    tiles_in = lax.all_to_all(pieces, "fsdp", split_axis=0, concat_axis=1, tiled=True).reshape(
        block_width, block_width
    )
    left_cols = tiles_in[:, :half_width]
    right_cols = tiles_in[:, half_width:]
    left_product = lax.dot_general(
        left_cols, whole_grad, contract_rows, preferred_element_type=jnp.float32
    ).astype(jnp.bfloat16)
    product = jnp.dot(left_product, right_cols, preferred_element_type=jnp.float32)
    own_block = jnp.arange(blocks) == block_pos
    update_square = jnp.where(own_block, jnp.sum(product * product), jnp.float32(0.0))
    grad_square, update_square = lax.psum((grad_square, update_square), "fsdp")
    graft_ratio = jnp.sqrt(grad_square) * lax.rsqrt(update_square + epsilon)
    scaled = (graft_ratio[block_pos] * product).astype(jnp.bfloat16)

    def send_tiles(outgoing_update):
        return lax.all_to_all(outgoing_update, "fsdp", split_axis=0, concat_axis=0, tiled=True)

    return tile_return(
        scaled, send_tiles, shard_count, shard_pos, part_index, blocks, row_count, half_width
    )


def schedule_kernel(packed_ref, table_ref, ahead, log):
    group_pos = lax.axis_index("group")
    lane = lax.broadcasted_iota(jnp.int32, (1, TILE), 1)
    node = lane % GROUPS
    rows = lax.broadcasted_iota(jnp.int32, (REACH, TILE), 0)
    packed = packed_ref[...]
    owner = jnp.where(packed < 0, -1, packed // 32)
    value = jnp.where(packed < 0, 0, packed % 32 + 1)
    for dist in range(1, GROUPS):
        shift = (TILE - dist) % TILE
        match = pltpu.roll(owner, shift, 1) == node
        line = jnp.max(jnp.where(match, pltpu.roll(value, shift, 1), 0), axis=0, keepdims=True)
        if dist <= REACH:
            near = jnp.where(line > 0, line + dist * 32, 0)
            if dist == REACH:
                near = jnp.where(node % 2 == 0, near, 0)
            ahead[0, dist - 1 : dist, :] = near
        if dist >= REACH:
            back = GROUPS - dist
            near = jnp.where(line > 0, line + back * 32, 0)
            if dist == REACH:
                near = jnp.where(node % 2 == 1, near, 0)
            ahead[1, back - 1 : back, :] = near

    def hop(index, carry):
        waiting, arrived, remain, whole = carry
        waiting, arrived = list(waiting), list(arrived)
        remain, whole = list(remain), list(whole)
        for train in range(TRAINS):
            place = index * TRAINS + train
            for way in range(2):
                at = train * 2 + way
                best = jnp.max(waiting[way], axis=0, keepdims=True)
                taken = jnp.logical_and(remain[at] == 0, best > 0)
                code = jnp.where(taken, best, 0)
                waiting[way] = jnp.where(waiting[way] == jnp.where(taken, best, -1), 0, waiting[way])
                log[pl.ds(way * STEPS + place, 1), :] = code % 32 - 1
                dist = code // 32
                left = jnp.where(taken, dist, remain[at])
                total = jnp.where(taken, dist, whole[at])
                shift = 1 if way == 0 else TILE - 1
                left = pltpu.roll(jnp.maximum(left - 1, 0), shift, 1)
                total = pltpu.roll(total, shift, 1)
                done = jnp.where(left == 0, total, 0)
                arrived[way] = jnp.where(rows + 1 == done, place, arrived[way])
                remain[at] = left
                whole[at] = jnp.where(left == 0, 0, total)
        return tuple(waiting), tuple(arrived), tuple(remain), tuple(whole)

    zero = jnp.zeros((1, TILE), jnp.int32)
    none = jnp.zeros((REACH, TILE), jnp.int32)
    start = (
        (ahead[0], ahead[1]),
        (none, none),
        (zero,) * (2 * TRAINS),
        (zero,) * (2 * TRAINS),
    )
    waiting, arrived, remain, _ = lax.fori_loop(0, HOPS, hop, start)
    log[DIST_ROWS : DIST_ROWS + REACH, :] = arrived[0]
    log[DIST_ROWS + REACH : OK_ROW, :] = arrived[1]
    open_count = jnp.max(jnp.maximum(waiting[0], waiting[1]), axis=0, keepdims=True)
    for count in remain:
        open_count = jnp.maximum(open_count, count)
    open_count = jnp.max(open_count, axis=1, keepdims=True)
    log[OK_ROW:TABLE_ROWS, :] = jnp.broadcast_to(open_count, (8, TILE))
    own = jnp.sum(jnp.where(lane == group_pos, log[...], 0), axis=1, keepdims=True)
    table_ref[...] = jnp.broadcast_to(own, (TABLE_ROWS, TILE))


def schedule(packed):
    lanes = jnp.tile(packed.T, (1, TILE // GROUPS))
    table = pl.pallas_call(
        schedule_kernel,
        out_shape=jax.ShapeDtypeStruct((TABLE_ROWS, TILE), jnp.int32),
        in_specs=[pl.BlockSpec(memory_space=pltpu.VMEM)],
        out_specs=pl.BlockSpec(memory_space=pltpu.VMEM),
        scratch_shapes=[
            pltpu.VMEM((2, REACH, TILE), jnp.int32),
            pltpu.VMEM((TABLE_ROWS, TILE), jnp.int32),
        ],
    )(lanes)
    return table[:, 0]


def turned(tile):
    return tile.astype(jnp.float32).T.astype(jnp.bfloat16)


def fill(inner, outer):
    for row in range(4):
        for col in range(row):
            inner[row * TILE : (row + 1) * TILE, col * TILE : (col + 1) * TILE] = turned(
                inner[col * TILE : (col + 1) * TILE, row * TILE : (row + 1) * TILE]
            )
        for col in range(row + 5, SUPER):
            away = row + SUPER - col - 1
            inner[row * TILE : (row + 1) * TILE, col * TILE : (col + 1) * TILE] = turned(
                outer[(col - 4) * TILE : (col - 3) * TILE, away * TILE : (away + 1) * TILE]
            )


def main_kernel(
    table, packed, grad, stale, fresh, out,
    fresh_band, stale_band, current, sending, log, whole_grad,
    left_in, left_out, right_in, right_out, left_product, product, tile, sums, sums_out,
    load_sem, ring_send, ring_recv, grad_send, grad_recv, left_send, left_recv,
    right_send, right_recv, sum_send, sum_recv, own_sem, tile_send, tile_recv,
):
    z = lax.axis_index("group")
    f = lax.axis_index("fsdp")
    onward = (lax.rem(z + 1, GROUPS), lax.rem(z + GROUPS - 1, GROUPS))
    superblock = f // 4
    block = f // 4
    part = lax.rem(f, 4)
    row_half = part // 2
    col_half = lax.rem(part, 2)

    loads = []
    for number, (source, target) in enumerate(((fresh, fresh_band), (stale, stale_band))):
        for col in range(5):
            start = pl.multiple_of(lax.rem(superblock + col, SUPER) * TILE, TILE)
            load = pltpu.make_async_copy(
                source.at[:, :, pl.ds(start, TILE)],
                target.at[:, :, pl.ds(col * TILE, TILE)],
                load_sem.at[number, col],
            )
            load.start()
            loads.append(load)

    barrier = pltpu.get_barrier_semaphore()
    for peer in onward:
        pl.semaphore_signal(barrier, inc=1, device_id=(peer, f), device_id_type=MESH)

    def greet(step, carry):
        peer = lax.rem(f + step, SHARDS)
        pl.semaphore_signal(barrier, inc=1, device_id=(z, peer), device_id_type=MESH)
        return carry

    lax.fori_loop(1, SHARDS, greet, 0)
    for load in loads:
        load.wait()
    pl.semaphore_wait(barrier, SHARDS + 1)

    def grad_copy(peer):
        row = lax.rem(f + SHARDS - 16 * (lax.rem(peer, 4) // 2), SHARDS)
        return (
            grad.at[peer // 4],
            whole_grad.at[pl.ds(pl.multiple_of(row * ROWS, ROWS), ROWS), :],
        )

    def grad_remote(peer):
        source, target = grad_copy(peer)
        return pltpu.make_async_remote_copy(
            src_ref=source, dst_ref=target, send_sem=grad_send.at[peer], recv_sem=grad_recv,
            device_id=(z, peer), device_id_type=MESH,
        )

    def each_peer(act):
        lax.fori_loop(1, SHARDS, lambda s, c: (act(lax.rem(f + s, SHARDS)), c)[1], 0)

    def ring_copy(way, index, train):
        turn = lax.rem(index, 3)
        return pltpu.make_async_remote_copy(
            src_ref=sending.at[(way * 3 + turn) * TRAINS + train],
            dst_ref=log.at[way * STEPS + index * TRAINS + train],
            send_sem=ring_send.at[way, turn, train],
            recv_sem=ring_recv.at[way, index, train],
            device_id=(onward[way], f),
            device_id_type=MESH,
        )

    def hop(index, first):
        for train in range(TRAINS):
            for way in range(2):
                place = index * TRAINS + train
                choice = table[way * STEPS + place]
                own = fresh_band[jnp.maximum(choice, 0)]
                turn = lax.rem(index, 3)
                if not first:
                    ring_copy(way, index - 1, train).wait_recv()

                    @pl.when(index >= 3)
                    def _():
                        ring_copy(way, index - 3, train).wait_send()

                    own = jnp.where(choice < 0, log[way * STEPS + place - TRAINS], own)
                sending[(way * 3 + turn) * TRAINS + train] = own
                ring_copy(way, index, train).start()

    hop(0, True)
    each_peer(lambda peer: grad_remote(peer).start())
    own_grad = pltpu.make_async_copy(*grad_copy(f), grad_recv)
    own_grad.start()
    lax.fori_loop(1, HOPS, lambda i, c: (hop(i, False), c)[1], 0)

    pltpu.make_async_copy(whole_grad, whole_grad, grad_recv).wait()

    def add_squares(index, total):
        rows = whole_grad[pl.ds(pl.multiple_of(index * 32, 32), 32), :].astype(jnp.float32)
        squares = (rows * rows).reshape(4, 8, 8, TILE)
        return total + jnp.sum(squares, axis=(0, 2))

    grad_square = lax.fori_loop(0, WIDTH // 32, add_squares, jnp.zeros((8, TILE), jnp.float32))

    for way in range(2):
        for train in range(TRAINS):
            ring_copy(way, HOPS - 1, train).wait_recv()
            for turn in range(3):
                ring_copy(way, HOPS - 3 + turn, train).wait_send()

    for root in range(ROOTS):
        code = packed[z * ROOTS + root]
        used = jnp.maximum(code, 0)
        owner = used // 32
        slot = lax.rem(used, 32)
        away = lax.rem(z - owner + GROUPS, GROUPS)
        ahead = jnp.logical_or(away < REACH, jnp.logical_and(away == REACH, lax.rem(owner, 2) == 0))
        dist = jnp.where(ahead, away, GROUPS - away)
        way = jnp.where(ahead, 0, 1)
        found = table[DIST_ROWS + way * REACH + jnp.maximum(dist - 1, 0)]
        moved = log[way * STEPS + found]
        own = jnp.where(away == 0, fresh_band[slot], moved)
        current[root] = jnp.where(code < 0, stale_band[root], own)

    def root_copies(number, half, peer_half, peer, inner, outer, send, recv, recv_out):
        place = lax.rem(f + SHARDS - 16 * peer_half, SHARDS)
        first_row = pl.multiple_of(lax.rem(place, 16) * ROWS, ROWS)
        col = pl.multiple_of(lax.rem(place // 4, 4) * TILE, TILE)
        near = (
            current.at[number],
            inner.at[pl.ds(first_row, ROWS), pl.ds(col, BAND)],
        )
        far = (
            current.at[number, :, pl.ds(TILE, REST)],
            outer.at[pl.ds(first_row, ROWS), :],
        )
        return place < 16, near, far

    def root_send(side, peer, wait):
        part = lax.rem(peer, 4)
        half = part // 2 if side == 0 else lax.rem(part, 2)
        number = (peer // 4) * 2 + side
        inner, outer, send, recv = (
            (left_in, left_out, left_send, left_recv),
            (right_in, right_out, right_send, right_recv),
        )[side]
        is_near, near, far = root_copies(number, 0, half, peer, inner, outer, send, recv, recv)

        def go(pair, sem):
            copy = pltpu.make_async_remote_copy(
                src_ref=pair[0], dst_ref=pair[1], send_sem=send.at[peer], recv_sem=sem,
                device_id=(z, peer), device_id_type=MESH,
            )
            if wait:
                copy.wait_send()
            else:
                copy.start()

        @pl.when(is_near)
        def _():
            go(near, recv.at[0])

        @pl.when(jnp.logical_not(is_near))
        def _():
            go(far, recv.at[1])

    def root_own(side):
        part = lax.rem(f, 4)
        half = part // 2 if side == 0 else lax.rem(part, 2)
        number = (f // 4) * 2 + side
        inner, outer, recv = ((left_in, left_out, left_recv), (right_in, right_out, right_recv))[side]
        is_near, near, far = root_copies(number, 0, half, f, inner, outer, None, None, None)

        @pl.when(is_near)
        def _():
            pltpu.make_async_copy(*near, recv.at[0]).start()

        @pl.when(jnp.logical_not(is_near))
        def _():
            pltpu.make_async_copy(*far, recv.at[1]).start()

    def root_wait(side):
        inner, outer, recv = ((left_in, left_out, left_recv), (right_in, right_out, right_recv))[side]
        window = inner.at[:, pl.ds(0, BAND)]
        pltpu.make_async_copy(window, window, recv.at[0]).wait()
        pltpu.make_async_copy(outer, outer, recv.at[1]).wait()

    for side in range(2):
        each_peer(functools.partial(root_send, side, wait=False))
        root_own(side)

    root_wait(0)
    fill(left_in, left_out)
    first_rows = pl.ds(0, HALF)

    def left_step(index, carry):
        cols = pl.ds(pl.multiple_of(index * 256, 256), 256)
        left_product[:, cols] = jnp.dot(
            left_in[...], whole_grad[:, cols], preferred_element_type=jnp.float32
        ).astype(jnp.bfloat16)
        return carry

    lax.fori_loop(0, 4, left_step, 0)
    root_wait(1)
    fill(right_in, right_out)
    near_cols = pl.ds(pl.multiple_of(col_half * HALF, HALF), HALF)
    far_cols = pl.ds(pl.multiple_of((1 - col_half) * HALF, HALF), HALF)
    contract_last = (((1,), (1,)), ((), ()))

    def right_step(index, total):
        rows = pl.ds(pl.multiple_of(index * TILE, TILE), TILE)
        value = lax.dot_general(
            left_product[rows, near_cols], right_in[:, :HALF], contract_last,
            preferred_element_type=jnp.float32,
        ) + lax.dot_general(
            left_product[rows, far_cols], right_in[:, HALF:], contract_last,
            preferred_element_type=jnp.float32,
        )
        product[rows, :] = value
        squares = (value * value).reshape(16, 8, 4, TILE)
        return total + jnp.sum(squares, axis=(0, 2))

    own_square = lax.fori_loop(0, 4, right_step, jnp.zeros((8, TILE), jnp.float32))
    sums_out[...] = own_square

    def sum_copy(step):
        peer = (f // 4) * 4 + lax.rem(part + step, 4)
        return pltpu.make_async_remote_copy(
            src_ref=sums_out, dst_ref=sums.at[part], send_sem=sum_send.at[step - 1],
            recv_sem=sum_recv, device_id=(z, peer), device_id_type=MESH,
        )

    for step in range(1, 4):
        sum_copy(step).start()
    pltpu.make_async_copy(sums_out, sums.at[part], sum_recv).start()
    pltpu.make_async_copy(sums, sums, sum_recv).wait()
    update_square = (sums[0] + sums[1]) + (sums[2] + sums[3])
    update_square = jnp.sum(update_square, axis=(0, 1), keepdims=True)
    grad_total = jnp.sum(grad_square, axis=(0, 1), keepdims=True)
    ratio = jnp.sqrt(grad_total) * lax.rsqrt(update_square + epsilon)

    def scale_step(index, carry):
        rows = pl.ds(pl.multiple_of(index * 64, 64), 64)
        tile[rows, :] = (ratio * product[rows, :]).astype(jnp.bfloat16)
        return carry

    lax.fori_loop(0, 8, scale_step, 0)

    def tile_copy(step):
        row = pl.multiple_of(step * ROWS, ROWS)
        return (
            tile.at[pl.ds(row, ROWS), :],
            out.at[block, :, pl.ds(pl.multiple_of(col_half * HALF, HALF), HALF)],
        )

    def tile_remote(step):
        source, target = tile_copy(step)
        return pltpu.make_async_remote_copy(
            src_ref=source, dst_ref=target, send_sem=tile_send.at[step], recv_sem=tile_recv,
            device_id=(z, row_half * 16 + step), device_id_type=MESH,
        )

    def tile_act(wait):
        def act(step, carry):
            turn = lax.rem(f + step, 16)

            @pl.when(row_half * 16 + turn != f)
            def _():
                copy = tile_remote(turn)
                if wait:
                    copy.wait_send()
                else:
                    copy.start()

            return carry

        lax.fori_loop(0, 16, act, 0)

    tile_act(False)

    @pl.when(row_half == f // 16)
    def _():
        pltpu.make_async_copy(*tile_copy(lax.rem(f, 16)), tile_recv).start()

    each_peer(lambda peer: grad_remote(peer).wait_send())
    for side in range(2):
        each_peer(functools.partial(root_send, side, wait=True))
    for step in range(1, 4):
        sum_copy(step).wait_send()
    tile_act(True)
    pltpu.make_async_copy(out, out, tile_recv).wait()


def ring_exchange(table, packed, grad_blocks, stale_roots, fresh_roots):
    bf16, f32 = jnp.bfloat16, jnp.float32
    dma = pltpu.SemaphoreType.DMA
    vmem = pltpu.VMEM
    smem_spec = pl.BlockSpec(memory_space=pltpu.SMEM)
    any_spec = pl.BlockSpec(memory_space=pl.ANY)
    vmem_spec = pl.BlockSpec(memory_space=pltpu.VMEM)
    return pl.pallas_call(
        main_kernel,
        out_shape=jax.ShapeDtypeStruct((BLOCKS, ROWS, WIDTH), bf16),
        in_specs=[smem_spec, smem_spec, vmem_spec, any_spec, any_spec],
        out_specs=vmem_spec,
        scratch_shapes=[
            vmem((ROOTS, ROWS, BAND), bf16),
            vmem((ROOTS, ROWS, BAND), bf16),
            vmem((ROOTS, ROWS, BAND), bf16),
            vmem((6 * TRAINS, ROWS, BAND), bf16),
            vmem((2 * STEPS, ROWS, BAND), bf16),
            vmem((WIDTH, WIDTH), bf16),
            vmem((HALF, WIDTH), bf16),
            vmem((HALF, REST), bf16),
            vmem((HALF, WIDTH), bf16),
            vmem((HALF, REST), bf16),
            vmem((HALF, WIDTH), bf16),
            vmem((HALF, HALF), f32),
            vmem((HALF, HALF), bf16),
            vmem((4, 8, TILE), f32),
            vmem((8, TILE), f32),
            dma((2, 5)),
            dma((2, 3, TRAINS)),
            dma((2, HOPS, TRAINS)),
            dma((SHARDS,)),
            dma(()),
            dma((SHARDS,)),
            dma((2,)),
            dma((SHARDS,)),
            dma((2,)),
            dma((3,)),
            dma(()),
            dma(()),
            dma((16,)),
            dma(()),
        ],
        compiler_params=pltpu.CompilerParams(
            collective_id=1, has_side_effects=True, vmem_limit_bytes=48 << 20
        ),
    )(table, packed, grad_blocks, stale_roots, fresh_roots)


def local(grad_blocks, stale_roots, fresh_roots, owner_list, slot_list, refresh_flags):
    packed = jnp.where(refresh_flags == 1, owner_list * 32 + slot_list, -1).astype(jnp.int32)
    table = schedule(packed)

    def by_ring(_):
        return ring_exchange(table, packed.reshape(-1), grad_blocks, stale_roots, fresh_roots)

    def by_all(_):
        return whole_exchange(
            grad_blocks, stale_roots, fresh_roots, owner_list, slot_list, refresh_flags
        )

    return lax.cond(table[OK_ROW] == 0, by_ring, by_all, None)


def solution(mesh):
    placed = (
        P("group", "fsdp", None),
        P("group", "fsdp", None),
        P("group", "fsdp", None),
        P(),
        P(),
        P(),
    )
    return jax.shard_map(
        local, mesh=mesh, in_specs=placed, out_specs=P("group", "fsdp", None), check_vma=False
    )
```

```python
import functools

import jax
import jax.numpy as jnp
from jax import lax
from jax.experimental import pallas as pl
from jax.experimental.pallas import tpu as pltpu
from jax.sharding import PartitionSpec as P

epsilon = 1e-06
MESH = pl.DeviceIdType.MESH
GROUPS = 32
SHARDS = 32
ROOTS = 16
BLOCKS = 8
ROWS = 32
WIDTH = 1024
HALF = 512
TILE = 128
SUPER = 8
BAND = 640
REST = 384
REACH = 16
HOPS = 18
TRAINS = 4
STEPS = HOPS * TRAINS
DIST_ROWS = 2 * STEPS
CODE_ROW = DIST_ROWS + 2 * REACH
OK_ROW = CODE_ROW + ROOTS
TABLE_ROWS = OK_ROW + 8


def tile_return(
    scaled, exchanged_fn, shard_count, shard_pos, part_index, blocks, row_count, half_width
):
    row_half = part_index // 2
    group_span = shard_count // 2
    keep_half = (jnp.arange(2) == row_half)[:, None, None, None]
    outgoing_update = jnp.where(
        keep_half, scaled.reshape(1, group_span, row_count, half_width), jnp.bfloat16(0.0)
    )
    outgoing_update = outgoing_update.reshape(shard_count, row_count, half_width)
    returned = exchanged_fn(outgoing_update)
    returned = returned.reshape(blocks, 2, 2, row_count, half_width)
    chosen = jnp.take(returned, shard_pos // group_span, axis=1)
    return chosen.transpose(0, 2, 1, 3).reshape(blocks, row_count, 2 * half_width)


def whole_exchange(grad_blocks, stale_roots, fresh_roots, owner_list, slot_list, refresh_flags):
    group_count = lax.axis_size("group")
    shard_count = lax.axis_size("fsdp")
    group_pos = lax.axis_index("group")
    shard_pos = lax.axis_index("fsdp")
    blocks, row_count, block_width = grad_blocks.shape
    roots_held = stale_roots.shape[0]
    half_width = block_width // 2
    flagged = refresh_flags == 1
    owned_here = jnp.logical_and(owner_list == group_pos, flagged)
    picked = jnp.sum(jnp.where(owned_here, slot_list, 0), axis=1)
    holding = jnp.any(owned_here, axis=1)
    selector = jnp.logical_and(
        picked[:, None] == jnp.arange(roots_held)[None, :], holding[:, None]
    ).astype(jnp.bfloat16)
    outgoing = jnp.einsum(
        "ts,sxw->txw", selector, fresh_roots, preferred_element_type=jnp.float32
    ).astype(jnp.bfloat16)
    arrived = lax.all_to_all(outgoing, "group", split_axis=0, concat_axis=0, tiled=True)
    own_owner = owner_list[group_pos]
    own_flag = flagged[group_pos]
    chooser = (own_owner[:, None] == jnp.arange(group_count)[None, :]).astype(jnp.bfloat16)
    delivered = jnp.einsum(
        "rt,txw->rxw", chooser, arrived, preferred_element_type=jnp.float32
    ).astype(jnp.bfloat16)
    current = jnp.where(own_flag[:, None, None], delivered, stale_roots)
    grad_square = jnp.sum(jnp.square(grad_blocks.astype(jnp.float32)), axis=(1, 2))
    spread = shard_count // blocks
    block_pos = shard_pos // spread
    part_index = shard_pos % spread
    left_roots = current[0::2]
    right_roots = current[1::2]
    contract_rows = (((0,), (0,)), ((), ()))
    tile_shape = (blocks, 2, 2, row_count, half_width)
    whole_grad = lax.all_to_all(
        jnp.repeat(grad_blocks, spread, axis=0), "fsdp", split_axis=0, concat_axis=1, tiled=True
    ).reshape(block_width, block_width)
    left_half = left_roots.reshape(blocks, row_count, 2, half_width).transpose(0, 2, 1, 3)
    right_half = right_roots.reshape(blocks, row_count, 2, half_width).transpose(0, 2, 1, 3)
    pieces = jnp.concatenate(
        [
            jnp.broadcast_to(left_half[:, :, None], tile_shape),
            jnp.broadcast_to(right_half[:, None], tile_shape),
        ],
        axis=4,
    ).reshape(shard_count, row_count, block_width)
    tiles_in = lax.all_to_all(pieces, "fsdp", split_axis=0, concat_axis=1, tiled=True).reshape(
        block_width, block_width
    )
    left_cols = tiles_in[:, :half_width]
    right_cols = tiles_in[:, half_width:]
    left_product = lax.dot_general(
        left_cols, whole_grad, contract_rows, preferred_element_type=jnp.float32
    ).astype(jnp.bfloat16)
    product = jnp.dot(left_product, right_cols, preferred_element_type=jnp.float32)
    own_block = jnp.arange(blocks) == block_pos
    update_square = jnp.where(own_block, jnp.sum(product * product), jnp.float32(0.0))
    grad_square, update_square = lax.psum((grad_square, update_square), "fsdp")
    graft_ratio = jnp.sqrt(grad_square) * lax.rsqrt(update_square + epsilon)
    scaled = (graft_ratio[block_pos] * product).astype(jnp.bfloat16)

    def send_tiles(outgoing_update):
        return lax.all_to_all(outgoing_update, "fsdp", split_axis=0, concat_axis=0, tiled=True)

    return tile_return(
        scaled, send_tiles, shard_count, shard_pos, part_index, blocks, row_count, half_width
    )


def schedule_kernel(owner_ref, slot_ref, flag_ref, table_ref, ahead, log):
    group_pos = lax.axis_index("group")
    lane = lax.broadcasted_iota(jnp.int32, (1, TILE), 1)
    node = lane % GROUPS
    rows = lax.broadcasted_iota(jnp.int32, (REACH, TILE), 0)
    packed = jnp.where(flag_ref[...] == 1, owner_ref[...] * 32 + slot_ref[...], -1)
    packed = jnp.concatenate([packed] * (TILE // GROUPS), axis=1)
    log[CODE_ROW:OK_ROW, :] = packed
    owner = jnp.where(packed < 0, -1, packed // 32)
    value = jnp.where(packed < 0, 0, packed % 32 + 1)
    for dist in range(1, GROUPS):
        shift = (TILE - dist) % TILE
        match = pltpu.roll(owner, shift, 1) == node
        line = jnp.max(jnp.where(match, pltpu.roll(value, shift, 1), 0), axis=0, keepdims=True)
        if dist <= REACH:
            near = jnp.where(line > 0, line + dist * 32, 0)
            if dist == REACH:
                near = jnp.where(node % 2 == 0, near, 0)
            ahead[0, dist - 1 : dist, :] = near
        if dist >= REACH:
            back = GROUPS - dist
            near = jnp.where(line > 0, line + back * 32, 0)
            if dist == REACH:
                near = jnp.where(node % 2 == 1, near, 0)
            ahead[1, back - 1 : back, :] = near

    def hop(index, carry):
        waiting, arrived, remain, whole = carry
        waiting, arrived = list(waiting), list(arrived)
        remain, whole = list(remain), list(whole)
        for train in range(TRAINS):
            place = index * TRAINS + train
            for way in range(2):
                at = train * 2 + way
                best = jnp.max(waiting[way], axis=0, keepdims=True)
                taken = jnp.logical_and(remain[at] == 0, best > 0)
                code = jnp.where(taken, best, 0)
                waiting[way] = jnp.where(waiting[way] == jnp.where(taken, best, -1), 0, waiting[way])
                log[pl.ds(way * STEPS + place, 1), :] = code % 32 - 1
                dist = code // 32
                left = jnp.where(taken, dist, remain[at])
                total = jnp.where(taken, dist, whole[at])
                shift = 1 if way == 0 else TILE - 1
                left = pltpu.roll(jnp.maximum(left - 1, 0), shift, 1)
                total = pltpu.roll(total, shift, 1)
                done = jnp.where(left == 0, total, 0)
                arrived[way] = jnp.where(rows + 1 == done, place, arrived[way])
                remain[at] = left
                whole[at] = jnp.where(left == 0, 0, total)
        return tuple(waiting), tuple(arrived), tuple(remain), tuple(whole)

    zero = jnp.zeros((1, TILE), jnp.int32)
    none = jnp.zeros((REACH, TILE), jnp.int32)
    start = (
        (ahead[0], ahead[1]),
        (none, none),
        (zero,) * (2 * TRAINS),
        (zero,) * (2 * TRAINS),
    )
    waiting, arrived, remain, _ = lax.fori_loop(0, HOPS, hop, start)
    log[DIST_ROWS : DIST_ROWS + REACH, :] = arrived[0]
    log[DIST_ROWS + REACH : CODE_ROW, :] = arrived[1]
    open_count = jnp.max(jnp.maximum(waiting[0], waiting[1]), axis=0, keepdims=True)
    for count in remain:
        open_count = jnp.maximum(open_count, count)
    open_count = jnp.max(open_count, axis=1, keepdims=True)
    log[OK_ROW:TABLE_ROWS, :] = jnp.broadcast_to(open_count, (8, TILE))
    own = jnp.sum(jnp.where(lane == group_pos, log[...], 0), axis=1, keepdims=True)
    table_ref[...] = jnp.broadcast_to(own, (TABLE_ROWS, TILE))


def schedule(owner_list, slot_list, refresh_flags):
    table = pl.pallas_call(
        schedule_kernel,
        out_shape=jax.ShapeDtypeStruct((TABLE_ROWS, TILE), jnp.int32),
        in_specs=[pl.BlockSpec(memory_space=pltpu.VMEM)] * 3,
        out_specs=pl.BlockSpec(memory_space=pltpu.VMEM),
        scratch_shapes=[
            pltpu.VMEM((2, REACH, TILE), jnp.int32),
            pltpu.VMEM((TABLE_ROWS, TILE), jnp.int32),
        ],
    )(owner_list.T, slot_list.T, refresh_flags.T)
    return table[:, 0]


def turned(tile):
    return tile.astype(jnp.float32).T.astype(jnp.bfloat16)


def fill_near(inner):
    for row in range(4):
        for col in range(row):
            inner[row * TILE : (row + 1) * TILE, col * TILE : (col + 1) * TILE] = turned(
                inner[col * TILE : (col + 1) * TILE, row * TILE : (row + 1) * TILE]
            )


def fill_far(inner, outer):
    for row in range(4):
        for col in range(row + 5, SUPER):
            away = row + SUPER - col - 1
            inner[row * TILE : (row + 1) * TILE, col * TILE : (col + 1) * TILE] = turned(
                outer[(col - 4) * TILE : (col - 3) * TILE, away * TILE : (away + 1) * TILE]
            )


def main_kernel(
    table, grad, stale, fresh, out,
    fresh_band, stale_band, current, sending, log, whole_grad,
    left_in, left_out, right_in, right_out, left_product, product, tile, tiles, sums, sums_out,
    load_sem, ring_send, ring_recv, grad_send, grad_recv, left_send, left_recv, left_pass,
    left_passed, right_send, right_recv, right_pass, right_passed, sum_send, sum_recv,
    tile_send, tile_recv,
):
    z = lax.axis_index("group")
    f = lax.axis_index("fsdp")
    onward = (lax.rem(z + 1, GROUPS), lax.rem(z + GROUPS - 1, GROUPS))
    superblock = f // 4
    block = f // 4
    place = lax.rem(f, 16)
    own_half = f // 16
    part = lax.rem(f, 4)
    row_half = part // 2
    col_half = lax.rem(part, 2)

    loads = []
    for number, (source, target) in enumerate(((fresh, fresh_band), (stale, stale_band))):
        for col in range(5):
            start = pl.multiple_of(lax.rem(superblock + col, SUPER) * TILE, TILE)
            load = pltpu.make_async_copy(
                source.at[:, :, pl.ds(start, TILE)],
                target.at[:, :, pl.ds(col * TILE, TILE)],
                load_sem.at[number, col],
            )
            load.start()
            loads.append(load)

    barrier = pltpu.get_barrier_semaphore()
    for peer in onward:
        pl.semaphore_signal(barrier, inc=1, device_id=(peer, f), device_id_type=MESH)

    def greet(step, carry):
        peer = lax.rem(f + step, SHARDS)
        pl.semaphore_signal(barrier, inc=1, device_id=(z, peer), device_id_type=MESH)
        return carry

    lax.fori_loop(1, SHARDS, greet, 0)
    for load in loads:
        load.wait()
    pl.semaphore_wait(barrier, SHARDS + 1)

    def grad_copy(peer):
        row = lax.rem(f + SHARDS - 16 * (lax.rem(peer, 4) // 2), SHARDS)
        return (
            grad.at[peer // 4],
            whole_grad.at[pl.ds(pl.multiple_of(row * ROWS, ROWS), ROWS), :],
        )

    def grad_remote(peer):
        source, target = grad_copy(peer)
        return pltpu.make_async_remote_copy(
            src_ref=source, dst_ref=target, send_sem=grad_send.at[peer], recv_sem=grad_recv,
            device_id=(z, peer), device_id_type=MESH,
        )

    def each_peer(act):
        lax.fori_loop(1, SHARDS, lambda s, c: (act(lax.rem(f + s, SHARDS)), c)[1], 0)

    def ring_copy(way, index, train):
        turn = lax.rem(index, 3)
        return pltpu.make_async_remote_copy(
            src_ref=sending.at[(way * 3 + turn) * TRAINS + train],
            dst_ref=log.at[way * STEPS + index * TRAINS + train],
            send_sem=ring_send.at[way, turn, train],
            recv_sem=ring_recv.at[way, index, train],
            device_id=(onward[way], f),
            device_id_type=MESH,
        )

    def hop(index, first):
        for train in range(TRAINS):
            for way in range(2):
                place = index * TRAINS + train
                choice = table[way * STEPS + place]
                own = fresh_band[jnp.maximum(choice, 0)]
                turn = lax.rem(index, 3)
                if not first:
                    ring_copy(way, index - 1, train).wait_recv()

                    @pl.when(index >= 3)
                    def _():
                        ring_copy(way, index - 3, train).wait_send()

                    own = jnp.where(choice < 0, log[way * STEPS + place - TRAINS], own)
                sending[(way * 3 + turn) * TRAINS + train] = own
                ring_copy(way, index, train).start()

    hop(0, True)
    each_peer(lambda peer: grad_remote(peer).start())
    own_grad = pltpu.make_async_copy(*grad_copy(f), grad_recv)
    own_grad.start()
    lax.fori_loop(1, HOPS, lambda i, c: (hop(i, False), c)[1], 0)

    pltpu.make_async_copy(whole_grad, whole_grad, grad_recv).wait()

    def add_squares(index, total):
        rows = whole_grad[pl.ds(pl.multiple_of(index * 32, 32), 32), :].astype(jnp.float32)
        squares = (rows * rows).reshape(4, 8, 8, TILE)
        return total + jnp.sum(squares, axis=(0, 2))

    grad_square = lax.fori_loop(0, WIDTH // 32, add_squares, jnp.zeros((8, TILE), jnp.float32))

    for way in range(2):
        for train in range(TRAINS):
            ring_copy(way, HOPS - 1, train).wait_recv()
            for turn in range(3):
                ring_copy(way, HOPS - 3 + turn, train).wait_send()

    def choose(root):
        code = table[CODE_ROW + root]
        used = jnp.maximum(code, 0)
        owner = used // 32
        slot = lax.rem(used, 32)
        away = lax.rem(z - owner + GROUPS, GROUPS)
        ahead = jnp.logical_or(away < REACH, jnp.logical_and(away == REACH, lax.rem(owner, 2) == 0))
        dist = jnp.where(ahead, away, GROUPS - away)
        way = jnp.where(ahead, 0, 1)
        found = table[DIST_ROWS + way * REACH + jnp.maximum(dist - 1, 0)]
        moved = log[way * STEPS + found]
        own = jnp.where(away == 0, fresh_band[slot], moved)
        current[root] = jnp.where(code < 0, stale_band[root], own)

    own_rows = pl.ds(pl.multiple_of(place * ROWS, ROWS), ROWS)
    own_band = pl.ds(pl.multiple_of((place // 4) * TILE, TILE), BAND)

    def deliver(source, target, peer, send_sem, recv_sem, wait):
        @pl.when(peer != f)
        def _():
            copy = pltpu.make_async_remote_copy(
                src_ref=source, dst_ref=target, send_sem=send_sem, recv_sem=recv_sem,
                device_id=(z, peer), device_id_type=MESH,
            )
            if wait:
                copy.wait_send()
            else:
                copy.start()

        if not wait:

            @pl.when(peer == f)
            def _():
                pltpu.make_async_copy(source, target, recv_sem).start()

    def left_send_step(step, wait):
        turn = lax.rem(f + step, 16)
        number = turn // 2
        half = lax.rem(turn, 2)
        peer = 4 * number + 2 * half + place // 8
        root = current.at[2 * number]

        @pl.when(half == own_half)
        def _():
            deliver(root, left_in.at[own_rows, own_band], peer, left_send.at[turn], left_recv.at[0], wait)

        @pl.when(half != own_half)
        def _():
            deliver(
                root.at[:, pl.ds(TILE, REST)], left_out.at[own_rows, :], peer,
                left_send.at[turn], left_recv.at[1], wait,
            )

    def right_send_step(step, wait):
        turn = lax.rem(f + step, 16)
        number = turn // 2
        peer = 4 * number + 2 * lax.rem(turn, 2) + own_half
        root = current.at[2 * number + 1]
        deliver(root, right_in.at[own_rows, own_band], peer, right_send.at[turn], right_recv, wait)

    def repeat(count, act):
        lax.fori_loop(0, count, lambda i, c: (act(i), c)[1], 0)

    for root in range(0, ROOTS, 2):
        choose(root)
    repeat(16, lambda step: left_send_step(step, False))
    for root in range(1, ROOTS, 2):
        choose(root)
    repeat(16, lambda step: right_send_step(step, False))

    sibling = f + 1 - 2 * col_half

    def hand(source, target, send_sem, recv_sem):
        return pltpu.make_async_remote_copy(
            src_ref=source, dst_ref=target, send_sem=send_sem, recv_sem=recv_sem,
            device_id=(z, sibling), device_id_type=MESH,
        )

    def await_bytes(window, sem):
        pltpu.make_async_copy(window, window, sem).wait()

    await_bytes(left_in.at[pl.ds(0, 256), pl.ds(0, BAND)], left_recv.at[0])
    await_bytes(left_out.at[pl.ds(0, 256), :], left_recv.at[1])
    hands = []
    for index in range(2):
        start = pl.multiple_of((2 * col_half + index) * TILE, TILE)
        window = left_in.at[pl.ds(start, TILE), pl.ds(start, BAND)]
        hands.append(hand(window, window, left_pass.at[index], left_passed))
    window = left_out.at[pl.ds(pl.multiple_of(256 * col_half, 256), 256), :]
    hands.append(hand(window, window, left_pass.at[2], left_passed))
    for copy in hands:
        copy.start()
    await_bytes(left_in.at[pl.ds(0, 256), :], left_passed)

    fill_near(left_in)
    fill_far(left_in, left_out)

    def left_step(index):
        cols = pl.ds(pl.multiple_of(index * 256, 256), 256)
        left_product[:, cols] = jnp.dot(
            left_in[...], whole_grad[:, cols], preferred_element_type=jnp.float32
        ).astype(jnp.bfloat16)

    repeat(4, left_step)

    await_bytes(right_in.at[:, pl.ds(0, BAND)], right_recv)
    for index in range(4):
        rows = pl.ds(index * TILE, TILE)
        source = right_in.at[rows, pl.ds((index + 1) * TILE, REST)]
        copy = hand(source, right_out.at[rows, :], right_pass.at[index], right_passed)
        copy.start()
        hands.append(copy)
    fill_near(right_in)
    near_cols = pl.ds(pl.multiple_of(col_half * HALF, HALF), HALF)
    next_cols = pl.ds(pl.multiple_of((1 - col_half) * HALF, HALF), TILE)
    last_cols = pl.ds(pl.multiple_of((1 - col_half) * HALF + TILE, TILE), REST)

    def times(rows, cols, start, size):
        return lax.dot_general(
            left_product[rows, cols], right_in[:, start : start + size], (((1,), (1,)), ((), ())),
            preferred_element_type=jnp.float32,
        )

    def near_step(index):
        rows = pl.ds(pl.multiple_of(index * TILE, TILE), TILE)
        product[rows, :] = times(rows, near_cols, 0, HALF) + times(rows, next_cols, HALF, TILE)

    repeat(4, near_step)
    await_bytes(right_out, right_passed)
    fill_far(right_in, right_out)

    def tile_step(chunk, index, wait):
        row = chunk * 4 + index
        deliver(
            tile.at[pl.ds(pl.multiple_of(row * ROWS, ROWS), ROWS), :],
            tiles.at[block, :, near_cols],
            row_half * 16 + row, tile_send.at[row], tile_recv, wait,
        )

    def last_step(index, total):
        chunk = lax.rem(index + block, 4)
        rows = pl.ds(pl.multiple_of(chunk * TILE, TILE), TILE)
        value = product[rows, :] + times(rows, last_cols, BAND, REST)
        tile[rows, :] = value.astype(jnp.bfloat16)
        repeat(4, lambda turn: tile_step(chunk, turn, False))
        squares = (value * value).reshape(16, 8, 4, TILE)
        return total + jnp.sum(squares, axis=(0, 2))

    update_part = lax.fori_loop(0, 4, last_step, jnp.zeros((8, TILE), jnp.float32))
    update_part = jnp.sum(update_part, axis=0, keepdims=True)
    grad_part = jnp.sum(grad_square, axis=0, keepdims=True)
    line = lax.broadcasted_iota(jnp.int32, (8, TILE), 0)
    sums_out[...] = jnp.where(line == 0, update_part, grad_part)

    def sum_step(step, wait):
        peer = lax.rem(f + step, SHARDS)
        deliver(sums_out, sums.at[f], peer, sum_send.at[step], sum_recv, wait)

    repeat(SHARDS, lambda step: sum_step(step, False))

    each_peer(lambda peer: grad_remote(peer).wait_send())
    repeat(16, lambda step: left_send_step(step, True))
    repeat(16, lambda step: right_send_step(step, True))
    for copy in hands:
        copy.wait_send()
    await_bytes(sums, sum_recv)
    ratios = []
    for number in range(BLOCKS):
        parts = [sums[4 * number + index] for index in range(4)]
        update_square = (parts[0] + parts[1]) + (parts[2] + parts[3])
        update_square = jnp.sum(update_square[0:1, :], axis=1, keepdims=True)
        grad_total = jnp.sum(parts[0][1:2, :], axis=1, keepdims=True)
        ratios.append(jnp.sqrt(grad_total) * lax.rsqrt(update_square + epsilon))
    await_bytes(tiles, tile_recv)
    for number in range(BLOCKS):
        out[number] = (ratios[number] * tiles[number].astype(jnp.float32)).astype(jnp.bfloat16)
    repeat(16, lambda row: tile_step(row // 4, lax.rem(row, 4), True))
    repeat(SHARDS, lambda step: sum_step(step, True))


def ring_exchange(table, grad_blocks, stale_roots, fresh_roots):
    bf16, f32 = jnp.bfloat16, jnp.float32
    dma = pltpu.SemaphoreType.DMA
    vmem = pltpu.VMEM
    smem_spec = pl.BlockSpec(memory_space=pltpu.SMEM)
    any_spec = pl.BlockSpec(memory_space=pl.ANY)
    vmem_spec = pl.BlockSpec(memory_space=pltpu.VMEM)
    return pl.pallas_call(
        main_kernel,
        out_shape=jax.ShapeDtypeStruct((BLOCKS, ROWS, WIDTH), bf16),
        in_specs=[smem_spec, vmem_spec, any_spec, any_spec],
        out_specs=vmem_spec,
        scratch_shapes=[
            vmem((ROOTS, ROWS, BAND), bf16),
            vmem((ROOTS, ROWS, BAND), bf16),
            vmem((ROOTS, ROWS, BAND), bf16),
            vmem((6 * TRAINS, ROWS, BAND), bf16),
            vmem((2 * STEPS, ROWS, BAND), bf16),
            vmem((WIDTH, WIDTH), bf16),
            vmem((HALF, WIDTH), bf16),
            vmem((HALF, REST), bf16),
            vmem((HALF, WIDTH), bf16),
            vmem((HALF, REST), bf16),
            vmem((HALF, WIDTH), bf16),
            vmem((HALF, HALF), f32),
            vmem((HALF, HALF), bf16),
            vmem((BLOCKS, ROWS, WIDTH), bf16),
            vmem((SHARDS, 8, TILE), f32),
            vmem((8, TILE), f32),
            dma((2, 5)),
            dma((2, 3, TRAINS)),
            dma((2, HOPS, TRAINS)),
            dma((SHARDS,)),
            dma(()),
            dma((16,)),
            dma((2,)),
            dma((3,)),
            dma(()),
            dma((16,)),
            dma(()),
            dma((4,)),
            dma(()),
            dma((SHARDS,)),
            dma(()),
            dma((16,)),
            dma(()),
        ],
        compiler_params=pltpu.CompilerParams(
            collective_id=1, has_side_effects=True, vmem_limit_bytes=48 << 20
        ),
    )(table, grad_blocks, stale_roots, fresh_roots)


def local(grad_blocks, stale_roots, fresh_roots, owner_list, slot_list, refresh_flags):
    table = schedule(owner_list, slot_list, refresh_flags)

    def by_ring(_):
        return ring_exchange(table, grad_blocks, stale_roots, fresh_roots)

    def by_all(_):
        return whole_exchange(
            grad_blocks, stale_roots, fresh_roots, owner_list, slot_list, refresh_flags
        )

    return lax.cond(table[OK_ROW] == 0, by_ring, by_all, None)


def solution(mesh):
    placed = (
        P("group", "fsdp", None),
        P("group", "fsdp", None),
        P("group", "fsdp", None),
        P(),
        P(),
        P(),
    )
    return jax.shard_map(
        local, mesh=mesh, in_specs=placed, out_specs=P("group", "fsdp", None), check_vma=False
    )
```

```python
import functools

import jax
import jax.numpy as jnp
from jax import lax
from jax.experimental import pallas as pl
from jax.experimental.pallas import tpu as pltpu
from jax.sharding import PartitionSpec as P

epsilon = 1e-06
MESH = pl.DeviceIdType.MESH
GROUPS = 32
SHARDS = 32
ROOTS = 16
BLOCKS = 8
ROWS = 32
WIDTH = 1024
HALF = 512
TILE = 128
SUPER = 8
BAND = 640
REST = 384
REACH = 16
HOPS = (16, 20)
MOST = HOPS[-1]
GRADS_A_HOP = 3
TRAINS = 4
STEPS = MOST * TRAINS
DIST_ROWS = 2 * STEPS
CODE_ROW = DIST_ROWS + 2 * REACH
NEED_ROW = CODE_ROW + ROOTS
TABLE_ROWS = NEED_ROW + 8


def tile_return(
    scaled, exchanged_fn, shard_count, shard_pos, part_index, blocks, row_count, half_width
):
    row_half = part_index // 2
    group_span = shard_count // 2
    keep_half = (jnp.arange(2) == row_half)[:, None, None, None]
    outgoing_update = jnp.where(
        keep_half, scaled.reshape(1, group_span, row_count, half_width), jnp.bfloat16(0.0)
    )
    outgoing_update = outgoing_update.reshape(shard_count, row_count, half_width)
    returned = exchanged_fn(outgoing_update)
    returned = returned.reshape(blocks, 2, 2, row_count, half_width)
    chosen = jnp.take(returned, shard_pos // group_span, axis=1)
    return chosen.transpose(0, 2, 1, 3).reshape(blocks, row_count, 2 * half_width)


def whole_exchange(grad_blocks, stale_roots, fresh_roots, owner_list, slot_list, refresh_flags):
    group_count = lax.axis_size("group")
    shard_count = lax.axis_size("fsdp")
    group_pos = lax.axis_index("group")
    shard_pos = lax.axis_index("fsdp")
    blocks, row_count, block_width = grad_blocks.shape
    roots_held = stale_roots.shape[0]
    half_width = block_width // 2
    flagged = refresh_flags == 1
    owned_here = jnp.logical_and(owner_list == group_pos, flagged)
    picked = jnp.sum(jnp.where(owned_here, slot_list, 0), axis=1)
    holding = jnp.any(owned_here, axis=1)
    selector = jnp.logical_and(
        picked[:, None] == jnp.arange(roots_held)[None, :], holding[:, None]
    ).astype(jnp.bfloat16)
    outgoing = jnp.einsum(
        "ts,sxw->txw", selector, fresh_roots, preferred_element_type=jnp.float32
    ).astype(jnp.bfloat16)
    arrived = lax.all_to_all(outgoing, "group", split_axis=0, concat_axis=0, tiled=True)
    own_owner = owner_list[group_pos]
    own_flag = flagged[group_pos]
    chooser = (own_owner[:, None] == jnp.arange(group_count)[None, :]).astype(jnp.bfloat16)
    delivered = jnp.einsum(
        "rt,txw->rxw", chooser, arrived, preferred_element_type=jnp.float32
    ).astype(jnp.bfloat16)
    current = jnp.where(own_flag[:, None, None], delivered, stale_roots)
    grad_square = jnp.sum(jnp.square(grad_blocks.astype(jnp.float32)), axis=(1, 2))
    spread = shard_count // blocks
    block_pos = shard_pos // spread
    part_index = shard_pos % spread
    left_roots = current[0::2]
    right_roots = current[1::2]
    contract_rows = (((0,), (0,)), ((), ()))
    tile_shape = (blocks, 2, 2, row_count, half_width)
    whole_grad = lax.all_to_all(
        jnp.repeat(grad_blocks, spread, axis=0), "fsdp", split_axis=0, concat_axis=1, tiled=True
    ).reshape(block_width, block_width)
    left_half = left_roots.reshape(blocks, row_count, 2, half_width).transpose(0, 2, 1, 3)
    right_half = right_roots.reshape(blocks, row_count, 2, half_width).transpose(0, 2, 1, 3)
    pieces = jnp.concatenate(
        [
            jnp.broadcast_to(left_half[:, :, None], tile_shape),
            jnp.broadcast_to(right_half[:, None], tile_shape),
        ],
        axis=4,
    ).reshape(shard_count, row_count, block_width)
    tiles_in = lax.all_to_all(pieces, "fsdp", split_axis=0, concat_axis=1, tiled=True).reshape(
        block_width, block_width
    )
    left_cols = tiles_in[:, :half_width]
    right_cols = tiles_in[:, half_width:]
    left_product = lax.dot_general(
        left_cols, whole_grad, contract_rows, preferred_element_type=jnp.float32
    ).astype(jnp.bfloat16)
    product = jnp.dot(left_product, right_cols, preferred_element_type=jnp.float32)
    own_block = jnp.arange(blocks) == block_pos
    update_square = jnp.where(own_block, jnp.sum(product * product), jnp.float32(0.0))
    grad_square, update_square = lax.psum((grad_square, update_square), "fsdp")
    graft_ratio = jnp.sqrt(grad_square) * lax.rsqrt(update_square + epsilon)
    scaled = (graft_ratio[block_pos] * product).astype(jnp.bfloat16)

    def send_tiles(outgoing_update):
        return lax.all_to_all(outgoing_update, "fsdp", split_axis=0, concat_axis=0, tiled=True)

    return tile_return(
        scaled, send_tiles, shard_count, shard_pos, part_index, blocks, row_count, half_width
    )


def schedule_kernel(owner_ref, slot_ref, flag_ref, table_ref, ahead, log):
    group_pos = lax.axis_index("group")
    lane = lax.broadcasted_iota(jnp.int32, (1, TILE), 1)
    node = lane % GROUPS
    rows = lax.broadcasted_iota(jnp.int32, (REACH, TILE), 0)
    packed = jnp.where(flag_ref[...] == 1, owner_ref[...] * 32 + slot_ref[...], -1)
    packed = jnp.concatenate([packed] * (TILE // GROUPS), axis=1)
    log[CODE_ROW:NEED_ROW, :] = packed
    for dist in range(1, GROUPS):
        seen = pltpu.roll(packed, (TILE - dist) % TILE, 1)
        match = jnp.right_shift(seen, 5) == node
        line = jnp.where(match, jnp.bitwise_and(seen, 31) + 1, 0)
        line = jnp.max(line, axis=0, keepdims=True)
        if dist <= REACH:
            near = jnp.where(line > 0, line + dist * 32, 0)
            if dist == REACH:
                near = jnp.where(node % 2 == 0, near, 0)
            ahead[0, dist - 1 : dist, :] = near
        if dist >= REACH:
            back = GROUPS - dist
            near = jnp.where(line > 0, line + back * 32, 0)
            if dist == REACH:
                near = jnp.where(node % 2 == 1, near, 0)
            ahead[1, back - 1 : back, :] = near

    def hop(index, carry):
        waiting, arrived, remain, whole = carry
        waiting, arrived = list(waiting), list(arrived)
        remain, whole = list(remain), list(whole)
        for train in range(TRAINS):
            place = index * TRAINS + train
            for way in range(2):
                at = train * 2 + way
                best = jnp.max(waiting[way], axis=0, keepdims=True)
                taken = jnp.logical_and(remain[at] == 0, best > 0)
                code = jnp.where(taken, best, 0)
                waiting[way] = jnp.where(waiting[way] == jnp.where(taken, best, -1), 0, waiting[way])
                log[pl.ds(way * STEPS + place, 1), :] = code % 32 - 1
                dist = code // 32
                left = jnp.where(taken, dist, remain[at])
                total = jnp.where(taken, dist, whole[at])
                shift = 1 if way == 0 else TILE - 1
                left = pltpu.roll(jnp.maximum(left - 1, 0), shift, 1)
                total = pltpu.roll(total, shift, 1)
                done = jnp.where(left == 0, total, 0)
                arrived[way] = jnp.where(rows + 1 == done, place, arrived[way])
                remain[at] = left
                whole[at] = jnp.where(left == 0, 0, total)
        return tuple(waiting), tuple(arrived), tuple(remain), tuple(whole)

    zero = jnp.zeros((1, TILE), jnp.int32)
    none = jnp.zeros((REACH, TILE), jnp.int32)
    start = (
        (ahead[0], ahead[1]),
        (none, none),
        (zero,) * (2 * TRAINS),
        (zero,) * (2 * TRAINS),
    )
    waiting, arrived, remain, _ = lax.fori_loop(0, MOST, hop, start)
    log[DIST_ROWS : DIST_ROWS + REACH, :] = arrived[0]
    log[DIST_ROWS + REACH : CODE_ROW, :] = arrived[1]
    open_count = jnp.max(jnp.maximum(waiting[0], waiting[1]), axis=0, keepdims=True)
    for count in remain:
        open_count = jnp.maximum(open_count, count)
    open_count = jnp.max(open_count, axis=1, keepdims=True)
    last = jnp.max(jnp.maximum(arrived[0], arrived[1]), axis=0, keepdims=True)
    need = jnp.max(last, axis=1, keepdims=True) // TRAINS + 1
    need = jnp.where(open_count > 0, MOST + 1, need)
    log[NEED_ROW:TABLE_ROWS, :] = jnp.broadcast_to(need, (8, TILE))
    own = jnp.sum(jnp.where(lane == group_pos, log[...], 0), axis=1, keepdims=True)
    table_ref[...] = jnp.broadcast_to(own, (TABLE_ROWS, TILE))


def schedule(owner_list, slot_list, refresh_flags):
    table = pl.pallas_call(
        schedule_kernel,
        out_shape=jax.ShapeDtypeStruct((TABLE_ROWS, TILE), jnp.int32),
        in_specs=[pl.BlockSpec(memory_space=pltpu.VMEM)] * 3,
        out_specs=pl.BlockSpec(memory_space=pltpu.VMEM),
        scratch_shapes=[
            pltpu.VMEM((2, REACH, TILE), jnp.int32),
            pltpu.VMEM((TABLE_ROWS, TILE), jnp.int32),
        ],
    )(owner_list.T, slot_list.T, refresh_flags.T)
    return table[:, 0]


def turned(tile):
    return tile.astype(jnp.float32).T.astype(jnp.bfloat16)


def fill_near(inner):
    for row in range(4):
        for col in range(row):
            inner[row * TILE : (row + 1) * TILE, col * TILE : (col + 1) * TILE] = turned(
                inner[col * TILE : (col + 1) * TILE, row * TILE : (row + 1) * TILE]
            )


def fill_far(inner, outer):
    for row in range(4):
        for col in range(row + 5, SUPER):
            away = row + SUPER - col - 1
            inner[row * TILE : (row + 1) * TILE, col * TILE : (col + 1) * TILE] = turned(
                outer[(col - 4) * TILE : (col - 3) * TILE, away * TILE : (away + 1) * TILE]
            )


def main_kernel(
    hops, table, grad, stale, fresh, out,
    fresh_band, stale_band, current, sending, log, whole_grad,
    left_in, left_out, right_in, right_out, left_product, product, tile, tiles, sums, sums_out,
    totals, totals_out,
    load_sem, ring_send, ring_recv, grad_send, grad_recv, left_send, left_recv, left_pass,
    left_passed, right_send, right_recv, right_pass, right_passed, sum_send, sum_recv,
    total_send, total_recv, tile_send, tile_recv,
):
    z = lax.axis_index("group")
    f = lax.axis_index("fsdp")
    onward = (lax.rem(z + 1, GROUPS), lax.rem(z + GROUPS - 1, GROUPS))
    superblock = f // 4
    block = f // 4
    place = lax.rem(f, 16)
    own_half = f // 16
    part = lax.rem(f, 4)
    row_half = part // 2
    col_half = lax.rem(part, 2)

    loads = []
    for number, (source, target) in enumerate(((fresh, fresh_band), (stale, stale_band))):
        for col in range(5):
            start = pl.multiple_of(lax.rem(superblock + col, SUPER) * TILE, TILE)
            load = pltpu.make_async_copy(
                source.at[:, :, pl.ds(start, TILE)],
                target.at[:, :, pl.ds(col * TILE, TILE)],
                load_sem.at[number, col],
            )
            load.start()
            loads.append(load)

    barrier = pltpu.get_barrier_semaphore()
    for peer in onward:
        pl.semaphore_signal(barrier, inc=1, device_id=(peer, f), device_id_type=MESH)

    def greet(step, carry):
        peer = lax.rem(f + step, SHARDS)
        pl.semaphore_signal(barrier, inc=1, device_id=(z, peer), device_id_type=MESH)
        return carry

    lax.fori_loop(1, SHARDS, greet, 0)
    for load in loads:
        load.wait()
    pl.semaphore_wait(barrier, SHARDS + 1)

    def grad_copy(peer):
        row = lax.rem(f + SHARDS - 16 * (lax.rem(peer, 4) // 2), SHARDS)
        return (
            grad.at[peer // 4],
            whole_grad.at[pl.ds(pl.multiple_of(row * ROWS, ROWS), ROWS), :],
        )

    def grad_remote(peer):
        source, target = grad_copy(peer)
        return pltpu.make_async_remote_copy(
            src_ref=source, dst_ref=target, send_sem=grad_send.at[peer], recv_sem=grad_recv,
            device_id=(z, peer), device_id_type=MESH,
        )

    def grad_step(index):
        @pl.when(index < SHARDS)
        def _():
            grad_remote(lax.rem(f + index, SHARDS)).start()

    def each_peer(act):
        lax.fori_loop(1, SHARDS, lambda s, c: (act(lax.rem(f + s, SHARDS)), c)[1], 0)

    def ring_copy(way, index, train):
        turn = lax.rem(index, 3)
        return pltpu.make_async_remote_copy(
            src_ref=sending.at[(way * 3 + turn) * TRAINS + train],
            dst_ref=log.at[way * STEPS + index * TRAINS + train],
            send_sem=ring_send.at[way, turn, train],
            recv_sem=ring_recv.at[way, index, train],
            device_id=(onward[way], f),
            device_id_type=MESH,
        )

    def hop(index, first):
        for train in range(TRAINS):
            for way in range(2):
                place = index * TRAINS + train
                choice = table[way * STEPS + place]
                own = fresh_band[jnp.maximum(choice, 0)]
                turn = lax.rem(index, 3)
                if not first:
                    ring_copy(way, index - 1, train).wait_recv()

                    @pl.when(index >= 3)
                    def _():
                        ring_copy(way, index - 3, train).wait_send()

                    own = jnp.where(choice < 0, log[way * STEPS + place - TRAINS], own)
                sending[(way * 3 + turn) * TRAINS + train] = own
                ring_copy(way, index, train).start()

    hop(0, True)
    own_grad = pltpu.make_async_copy(*grad_copy(f), grad_recv)
    own_grad.start()

    def hop_and_grads(index, carry):
        hop(index, False)
        for extra in range(GRADS_A_HOP):
            grad_step((index - 1) * GRADS_A_HOP + 1 + extra)
        return carry

    lax.fori_loop(1, hops, hop_and_grads, 0)

    for way in range(2):
        for train in range(TRAINS):
            ring_copy(way, hops - 1, train).wait_recv()
            for turn in range(3):
                ring_copy(way, hops - 3 + turn, train).wait_send()

    def choose(root):
        code = table[CODE_ROW + root]
        used = jnp.maximum(code, 0)
        owner = used // 32
        slot = lax.rem(used, 32)
        away = lax.rem(z - owner + GROUPS, GROUPS)
        ahead = jnp.logical_or(away < REACH, jnp.logical_and(away == REACH, lax.rem(owner, 2) == 0))
        dist = jnp.where(ahead, away, GROUPS - away)
        way = jnp.where(ahead, 0, 1)
        found = table[DIST_ROWS + way * REACH + jnp.maximum(dist - 1, 0)]
        moved = log[way * STEPS + found]
        own = jnp.where(away == 0, fresh_band[slot], moved)
        current[root] = jnp.where(code < 0, stale_band[root], own)

    own_rows = pl.ds(pl.multiple_of(place * ROWS, ROWS), ROWS)
    own_band = pl.ds(pl.multiple_of((place // 4) * TILE, TILE), BAND)

    def deliver(source, target, peer, send_sem, recv_sem, wait):
        @pl.when(peer != f)
        def _():
            copy = pltpu.make_async_remote_copy(
                src_ref=source, dst_ref=target, send_sem=send_sem, recv_sem=recv_sem,
                device_id=(z, peer), device_id_type=MESH,
            )
            if wait:
                copy.wait_send()
            else:
                copy.start()

        if not wait:

            @pl.when(peer == f)
            def _():
                pltpu.make_async_copy(source, target, recv_sem).start()

    def left_send_step(step, wait):
        turn = lax.rem(f + step, 16)
        number = turn // 2
        half = lax.rem(turn, 2)
        peer = 4 * number + 2 * half + place // 8
        root = current.at[2 * number]

        @pl.when(half == own_half)
        def _():
            deliver(root, left_in.at[own_rows, own_band], peer, left_send.at[turn], left_recv.at[0], wait)

        @pl.when(half != own_half)
        def _():
            deliver(
                root.at[:, pl.ds(TILE, REST)], left_out.at[own_rows, :], peer,
                left_send.at[turn], left_recv.at[1], wait,
            )

    def right_send_step(step, wait):
        turn = lax.rem(f + step, 16)
        number = turn // 2
        peer = 4 * number + 2 * lax.rem(turn, 2) + own_half
        root = current.at[2 * number + 1]
        deliver(root, right_in.at[own_rows, own_band], peer, right_send.at[turn], right_recv, wait)

    def repeat(count, act):
        lax.fori_loop(0, count, lambda i, c: (act(i), c)[1], 0)

    for root in range(0, ROOTS, 2):
        choose(root)
    repeat(16, lambda step: left_send_step(step, False))
    for root in range(1, ROOTS, 2):
        choose(root)
    repeat(16, lambda step: right_send_step(step, False))

    sibling = f + 1 - 2 * col_half

    def hand(source, target, send_sem, recv_sem):
        return pltpu.make_async_remote_copy(
            src_ref=source, dst_ref=target, send_sem=send_sem, recv_sem=recv_sem,
            device_id=(z, sibling), device_id_type=MESH,
        )

    def await_bytes(window, sem):
        pltpu.make_async_copy(window, window, sem).wait()

    pltpu.make_async_copy(whole_grad, whole_grad, grad_recv).wait()

    def add_squares(index, total):
        rows = whole_grad[pl.ds(pl.multiple_of(index * 32, 32), 32), :].astype(jnp.float32)
        squares = (rows * rows).reshape(4, 8, 8, TILE)
        return total + jnp.sum(squares, axis=(0, 2))

    grad_square = lax.fori_loop(0, WIDTH // 32, add_squares, jnp.zeros((8, TILE), jnp.float32))

    await_bytes(left_in.at[pl.ds(0, 256), pl.ds(0, BAND)], left_recv.at[0])
    await_bytes(left_out.at[pl.ds(0, 256), :], left_recv.at[1])
    hands = []
    for index in range(2):
        start = pl.multiple_of((2 * col_half + index) * TILE, TILE)
        window = left_in.at[pl.ds(start, TILE), pl.ds(start, BAND)]
        hands.append(hand(window, window, left_pass.at[index], left_passed))
    window = left_out.at[pl.ds(pl.multiple_of(256 * col_half, 256), 256), :]
    hands.append(hand(window, window, left_pass.at[2], left_passed))
    for copy in hands:
        copy.start()
    await_bytes(left_in.at[pl.ds(0, 256), :], left_passed)

    fill_near(left_in)
    fill_far(left_in, left_out)

    def left_step(index):
        cols = pl.ds(pl.multiple_of(index * 256, 256), 256)
        left_product[:, cols] = jnp.dot(
            left_in[...], whole_grad[:, cols], preferred_element_type=jnp.float32
        ).astype(jnp.bfloat16)

    repeat(4, left_step)

    await_bytes(right_in.at[:, pl.ds(0, BAND)], right_recv)
    for index in range(4):
        rows = pl.ds(index * TILE, TILE)
        source = right_in.at[rows, pl.ds((index + 1) * TILE, REST)]
        copy = hand(source, right_out.at[rows, :], right_pass.at[index], right_passed)
        copy.start()
        hands.append(copy)
    fill_near(right_in)
    near_cols = pl.ds(pl.multiple_of(col_half * HALF, HALF), HALF)
    next_cols = pl.ds(pl.multiple_of((1 - col_half) * HALF, HALF), TILE)
    last_cols = pl.ds(pl.multiple_of((1 - col_half) * HALF + TILE, TILE), REST)

    def times(rows, cols, start, size):
        return lax.dot_general(
            left_product[rows, cols], right_in[:, start : start + size], (((1,), (1,)), ((), ())),
            preferred_element_type=jnp.float32,
        )

    def near_step(index):
        rows = pl.ds(pl.multiple_of(index * TILE, TILE), TILE)
        product[rows, :] = times(rows, near_cols, 0, HALF) + times(rows, next_cols, HALF, TILE)

    repeat(4, near_step)
    await_bytes(right_out, right_passed)
    fill_far(right_in, right_out)

    def tile_step(row, wait):
        deliver(
            tile.at[pl.ds(pl.multiple_of(row * ROWS, ROWS), ROWS), :],
            tiles.at[block, :, near_cols],
            row_half * 16 + row, tile_send.at[row], tile_recv, wait,
        )

    def last_step(index, total):
        rows = pl.ds(pl.multiple_of(index * TILE, TILE), TILE)
        value = product[rows, :] + times(rows, last_cols, BAND, REST)
        tile[rows, :] = value.astype(jnp.bfloat16)
        squares = (value * value).reshape(16, 8, 4, TILE)
        return total + jnp.sum(squares, axis=(0, 2))

    update_part = lax.fori_loop(0, 4, last_step, jnp.zeros((8, TILE), jnp.float32))
    update_part = jnp.sum(update_part, axis=0, keepdims=True)
    grad_part = jnp.sum(grad_square, axis=0, keepdims=True)
    line = lax.broadcasted_iota(jnp.int32, (8, TILE), 0)
    sums_out[...] = jnp.where(line == 0, update_part, grad_part)

    def sum_step(step, wait):
        peer = 4 * block + lax.rem(part + step, 4)
        deliver(sums_out, sums.at[part], peer, sum_send.at[step], sum_recv, wait)

    def total_step(step, wait):
        peer = row_half * 16 + 2 * lax.rem(step + block, 8) + col_half
        deliver(totals_out, totals.at[block], peer, total_send.at[step], total_recv, wait)

    repeat(4, lambda step: sum_step(step, False))
    repeat(16, lambda step: tile_step(lax.rem(step + 4 * block, 16), False))
    await_bytes(sums, sum_recv)
    update_part = (sums[0] + sums[1]) + (sums[2] + sums[3])
    totals_out[...] = jnp.where(line == 0, update_part, grad_part)
    repeat(8, lambda step: total_step(step, False))

    each_peer(lambda peer: grad_remote(peer).wait_send())
    repeat(16, lambda step: left_send_step(step, True))
    repeat(16, lambda step: right_send_step(step, True))
    for copy in hands:
        copy.wait_send()
    await_bytes(totals, total_recv)
    ratios = []
    for number in range(BLOCKS):
        update_square = jnp.sum(totals[number, 0:1, :], axis=1, keepdims=True)
        grad_total = jnp.sum(totals[number, 1:2, :], axis=1, keepdims=True)
        ratios.append(jnp.sqrt(grad_total) * lax.rsqrt(update_square + epsilon))
    await_bytes(tiles, tile_recv)
    for number in range(BLOCKS):
        out[number] = (ratios[number] * tiles[number].astype(jnp.float32)).astype(jnp.bfloat16)
    repeat(16, lambda row: tile_step(row, True))
    repeat(4, lambda step: sum_step(step, True))
    repeat(8, lambda step: total_step(step, True))


def ring_exchange(hops, table, grad_blocks, stale_roots, fresh_roots):
    bf16, f32 = jnp.bfloat16, jnp.float32
    dma = pltpu.SemaphoreType.DMA
    vmem = pltpu.VMEM
    smem_spec = pl.BlockSpec(memory_space=pltpu.SMEM)
    any_spec = pl.BlockSpec(memory_space=pl.ANY)
    vmem_spec = pl.BlockSpec(memory_space=pltpu.VMEM)
    return pl.pallas_call(
        functools.partial(main_kernel, hops),
        out_shape=jax.ShapeDtypeStruct((BLOCKS, ROWS, WIDTH), bf16),
        in_specs=[smem_spec, any_spec, any_spec, any_spec],
        out_specs=vmem_spec,
        scratch_shapes=[
            vmem((ROOTS, ROWS, BAND), bf16),
            vmem((ROOTS, ROWS, BAND), bf16),
            vmem((ROOTS, ROWS, BAND), bf16),
            vmem((6 * TRAINS, ROWS, BAND), bf16),
            vmem((2 * STEPS, ROWS, BAND), bf16),
            vmem((WIDTH, WIDTH), bf16),
            vmem((HALF, WIDTH), bf16),
            vmem((HALF, REST), bf16),
            vmem((HALF, WIDTH), bf16),
            vmem((HALF, REST), bf16),
            vmem((HALF, WIDTH), bf16),
            vmem((HALF, HALF), f32),
            vmem((HALF, HALF), bf16),
            vmem((BLOCKS, ROWS, WIDTH), bf16),
            vmem((4, 8, TILE), f32),
            vmem((8, TILE), f32),
            vmem((BLOCKS, 8, TILE), f32),
            vmem((8, TILE), f32),
            dma((2, 5)),
            dma((2, 3, TRAINS)),
            dma((2, hops, TRAINS)),
            dma((SHARDS,)),
            dma(()),
            dma((16,)),
            dma((2,)),
            dma((3,)),
            dma(()),
            dma((16,)),
            dma(()),
            dma((4,)),
            dma(()),
            dma((4,)),
            dma(()),
            dma((8,)),
            dma(()),
            dma((16,)),
            dma(()),
        ],
        compiler_params=pltpu.CompilerParams(
            collective_id=HOPS.index(hops), has_side_effects=True, vmem_limit_bytes=48 << 20
        ),
    )(table, grad_blocks, stale_roots, fresh_roots)


def local(grad_blocks, stale_roots, fresh_roots, owner_list, slot_list, refresh_flags):
    table = schedule(owner_list, slot_list, refresh_flags)

    def by_ring(hops):
        return lambda _: ring_exchange(hops, table, grad_blocks, stale_roots, fresh_roots)

    def by_all(_):
        return whole_exchange(
            grad_blocks, stale_roots, fresh_roots, owner_list, slot_list, refresh_flags
        )

    need = table[NEED_ROW]
    path = sum((need > hops).astype(jnp.int32) for hops in HOPS)
    return lax.switch(path, [by_ring(hops) for hops in HOPS] + [by_all], None)


def solution(mesh):
    placed = (
        P("group", "fsdp", None),
        P("group", "fsdp", None),
        P("group", "fsdp", None),
        P(),
        P(),
        P(),
    )
    return jax.shard_map(
        local, mesh=mesh, in_specs=placed, out_specs=P("group", "fsdp", None), check_vma=False
    )
```

```python
import functools

import jax
import jax.numpy as jnp
from jax import lax
from jax.experimental import pallas as pl
from jax.experimental.pallas import tpu as pltpu
from jax.sharding import PartitionSpec as P

epsilon = 1e-06
MESH = pl.DeviceIdType.MESH
GROUPS = 32
SHARDS = 32
ROOTS = 16
BLOCKS = 8
ROWS = 32
WIDTH = 1024
HALF = 512
TILE = 128
SUPER = 8
BAND = 640
REST = 384
REACH = 16
HOPS = (16, 20)
MOST = HOPS[-1]
GRADS_A_HOP = 3
TRAINS = 4
STEPS = MOST * TRAINS
DIST_ROWS = 2 * STEPS
CODE_ROW = DIST_ROWS + 2 * REACH
NEED_ROW = CODE_ROW + ROOTS
TABLE_ROWS = NEED_ROW + 8


def tile_return(
    scaled, exchanged_fn, shard_count, shard_pos, part_index, blocks, row_count, half_width
):
    row_half = part_index // 2
    group_span = shard_count // 2
    keep_half = (jnp.arange(2) == row_half)[:, None, None, None]
    outgoing_update = jnp.where(
        keep_half, scaled.reshape(1, group_span, row_count, half_width), jnp.bfloat16(0.0)
    )
    outgoing_update = outgoing_update.reshape(shard_count, row_count, half_width)
    returned = exchanged_fn(outgoing_update)
    returned = returned.reshape(blocks, 2, 2, row_count, half_width)
    chosen = jnp.take(returned, shard_pos // group_span, axis=1)
    return chosen.transpose(0, 2, 1, 3).reshape(blocks, row_count, 2 * half_width)


def whole_exchange(grad_blocks, stale_roots, fresh_roots, owner_list, slot_list, refresh_flags):
    group_count = lax.axis_size("group")
    shard_count = lax.axis_size("fsdp")
    group_pos = lax.axis_index("group")
    shard_pos = lax.axis_index("fsdp")
    blocks, row_count, block_width = grad_blocks.shape
    roots_held = stale_roots.shape[0]
    half_width = block_width // 2
    flagged = refresh_flags == 1
    owned_here = jnp.logical_and(owner_list == group_pos, flagged)
    picked = jnp.sum(jnp.where(owned_here, slot_list, 0), axis=1)
    holding = jnp.any(owned_here, axis=1)
    selector = jnp.logical_and(
        picked[:, None] == jnp.arange(roots_held)[None, :], holding[:, None]
    ).astype(jnp.bfloat16)
    outgoing = jnp.einsum(
        "ts,sxw->txw", selector, fresh_roots, preferred_element_type=jnp.float32
    ).astype(jnp.bfloat16)
    arrived = lax.all_to_all(outgoing, "group", split_axis=0, concat_axis=0, tiled=True)
    own_owner = owner_list[group_pos]
    own_flag = flagged[group_pos]
    chooser = (own_owner[:, None] == jnp.arange(group_count)[None, :]).astype(jnp.bfloat16)
    delivered = jnp.einsum(
        "rt,txw->rxw", chooser, arrived, preferred_element_type=jnp.float32
    ).astype(jnp.bfloat16)
    current = jnp.where(own_flag[:, None, None], delivered, stale_roots)
    grad_square = jnp.sum(jnp.square(grad_blocks.astype(jnp.float32)), axis=(1, 2))
    spread = shard_count // blocks
    block_pos = shard_pos // spread
    part_index = shard_pos % spread
    left_roots = current[0::2]
    right_roots = current[1::2]
    contract_rows = (((0,), (0,)), ((), ()))
    tile_shape = (blocks, 2, 2, row_count, half_width)
    whole_grad = lax.all_to_all(
        jnp.repeat(grad_blocks, spread, axis=0), "fsdp", split_axis=0, concat_axis=1, tiled=True
    ).reshape(block_width, block_width)
    left_half = left_roots.reshape(blocks, row_count, 2, half_width).transpose(0, 2, 1, 3)
    right_half = right_roots.reshape(blocks, row_count, 2, half_width).transpose(0, 2, 1, 3)
    pieces = jnp.concatenate(
        [
            jnp.broadcast_to(left_half[:, :, None], tile_shape),
            jnp.broadcast_to(right_half[:, None], tile_shape),
        ],
        axis=4,
    ).reshape(shard_count, row_count, block_width)
    tiles_in = lax.all_to_all(pieces, "fsdp", split_axis=0, concat_axis=1, tiled=True).reshape(
        block_width, block_width
    )
    left_cols = tiles_in[:, :half_width]
    right_cols = tiles_in[:, half_width:]
    left_product = lax.dot_general(
        left_cols, whole_grad, contract_rows, preferred_element_type=jnp.float32
    ).astype(jnp.bfloat16)
    product = jnp.dot(left_product, right_cols, preferred_element_type=jnp.float32)
    own_block = jnp.arange(blocks) == block_pos
    update_square = jnp.where(own_block, jnp.sum(product * product), jnp.float32(0.0))
    grad_square, update_square = lax.psum((grad_square, update_square), "fsdp")
    graft_ratio = jnp.sqrt(grad_square) * lax.rsqrt(update_square + epsilon)
    scaled = (graft_ratio[block_pos] * product).astype(jnp.bfloat16)

    def send_tiles(outgoing_update):
        return lax.all_to_all(outgoing_update, "fsdp", split_axis=0, concat_axis=0, tiled=True)

    return tile_return(
        scaled, send_tiles, shard_count, shard_pos, part_index, blocks, row_count, half_width
    )


def schedule_kernel(owner_ref, slot_ref, flag_ref, table_ref, ahead, log):
    group_pos = lax.axis_index("group")
    lane = lax.broadcasted_iota(jnp.int32, (1, TILE), 1)
    node = lane % GROUPS
    rows = lax.broadcasted_iota(jnp.int32, (REACH, TILE), 0)
    packed = jnp.where(flag_ref[...] == 1, owner_ref[...] * 32 + slot_ref[...], -1)
    packed = jnp.concatenate([packed] * (TILE // GROUPS), axis=1)
    log[CODE_ROW:NEED_ROW, :] = packed
    for dist in range(1, GROUPS):
        seen = pltpu.roll(packed, (TILE - dist) % TILE, 1)
        match = jnp.right_shift(seen, 5) == node
        line = jnp.where(match, jnp.bitwise_and(seen, 31) + 1, 0)
        line = jnp.max(line, axis=0, keepdims=True)
        if dist <= REACH:
            near = jnp.where(line > 0, line + dist * 32, 0)
            if dist == REACH:
                near = jnp.where(node % 2 == 0, near, 0)
            ahead[0, dist - 1 : dist, :] = near
        if dist >= REACH:
            back = GROUPS - dist
            near = jnp.where(line > 0, line + back * 32, 0)
            if dist == REACH:
                near = jnp.where(node % 2 == 1, near, 0)
            ahead[1, back - 1 : back, :] = near

    def hop(index, carry):
        waiting, arrived, remain, whole = carry
        waiting, arrived = list(waiting), list(arrived)
        remain, whole = list(remain), list(whole)
        for train in range(TRAINS):
            place = index * TRAINS + train
            for way in range(2):
                at = train * 2 + way
                best = jnp.max(waiting[way], axis=0, keepdims=True)
                taken = jnp.logical_and(remain[at] == 0, best > 0)
                code = jnp.where(taken, best, 0)
                waiting[way] = jnp.where(waiting[way] == jnp.where(taken, best, -1), 0, waiting[way])
                log[pl.ds(way * STEPS + place, 1), :] = code % 32 - 1
                dist = code // 32
                left = jnp.where(taken, dist, remain[at])
                total = jnp.where(taken, dist, whole[at])
                shift = 1 if way == 0 else TILE - 1
                left = pltpu.roll(jnp.maximum(left - 1, 0), shift, 1)
                total = pltpu.roll(total, shift, 1)
                done = jnp.where(left == 0, total, 0)
                arrived[way] = jnp.where(rows + 1 == done, place, arrived[way])
                remain[at] = left
                whole[at] = jnp.where(left == 0, 0, total)
        return tuple(waiting), tuple(arrived), tuple(remain), tuple(whole)

    zero = jnp.zeros((1, TILE), jnp.int32)
    none = jnp.zeros((REACH, TILE), jnp.int32)
    start = (
        (ahead[0], ahead[1]),
        (none, none),
        (zero,) * (2 * TRAINS),
        (zero,) * (2 * TRAINS),
    )
    waiting, arrived, remain, _ = lax.fori_loop(0, MOST, hop, start)
    log[DIST_ROWS : DIST_ROWS + REACH, :] = arrived[0]
    log[DIST_ROWS + REACH : CODE_ROW, :] = arrived[1]
    open_count = jnp.max(jnp.maximum(waiting[0], waiting[1]), axis=0, keepdims=True)
    for count in remain:
        open_count = jnp.maximum(open_count, count)
    open_count = jnp.max(open_count, axis=1, keepdims=True)
    last = jnp.max(jnp.maximum(arrived[0], arrived[1]), axis=0, keepdims=True)
    need = jnp.max(last, axis=1, keepdims=True) // TRAINS + 1
    need = jnp.where(open_count > 0, MOST + 1, need)
    log[NEED_ROW:TABLE_ROWS, :] = jnp.broadcast_to(need, (8, TILE))
    own = jnp.sum(jnp.where(lane == group_pos, log[...], 0), axis=1, keepdims=True)
    table_ref[...] = jnp.broadcast_to(own, (TABLE_ROWS, TILE))


def schedule(owner_list, slot_list, refresh_flags):
    table = pl.pallas_call(
        schedule_kernel,
        out_shape=jax.ShapeDtypeStruct((TABLE_ROWS, TILE), jnp.int32),
        in_specs=[pl.BlockSpec(memory_space=pltpu.VMEM)] * 3,
        out_specs=pl.BlockSpec(memory_space=pltpu.VMEM),
        scratch_shapes=[
            pltpu.VMEM((2, REACH, TILE), jnp.int32),
            pltpu.VMEM((TABLE_ROWS, TILE), jnp.int32),
        ],
    )(owner_list.T, slot_list.T, refresh_flags.T)
    return table[:, 0]


def turned(tile):
    return tile.astype(jnp.float32).T.astype(jnp.bfloat16)


def fill_near(inner):
    for row in range(4):
        for col in range(row):
            inner[row * TILE : (row + 1) * TILE, col * TILE : (col + 1) * TILE] = turned(
                inner[col * TILE : (col + 1) * TILE, row * TILE : (row + 1) * TILE]
            )


def fill_far(inner, outer):
    for row in range(4):
        for col in range(row + 5, SUPER):
            away = row + SUPER - col - 1
            inner[row * TILE : (row + 1) * TILE, col * TILE : (col + 1) * TILE] = turned(
                outer[(col - 4) * TILE : (col - 3) * TILE, away * TILE : (away + 1) * TILE]
            )


def main_kernel(
    hops, table, grad, stale, fresh, out,
    fresh_band, stale_band, current, sending, log, whole_grad,
    left_in, left_out, right_in, right_out, left_product, product, tile, tiles, sums, sums_out,
    totals, totals_out,
    load_sem, ring_send, ring_recv, grad_send, grad_recv, left_send, left_recv, left_pass,
    left_passed, right_send, right_recv, right_pass, right_passed, sum_send, sum_recv,
    total_send, total_recv, tile_send, tile_recv,
):
    z = lax.axis_index("group")
    f = lax.axis_index("fsdp")
    onward = (lax.rem(z + 1, GROUPS), lax.rem(z + GROUPS - 1, GROUPS))
    superblock = f // 4
    block = f // 4
    place = lax.rem(f, 16)
    own_half = f // 16
    part = lax.rem(f, 4)
    row_half = part // 2
    col_half = lax.rem(part, 2)

    barrier = pltpu.get_barrier_semaphore()
    for peer in onward:
        pl.semaphore_signal(barrier, inc=1, device_id=(peer, f), device_id_type=MESH)

    def greet(step, carry):
        peer = lax.rem(f + step, SHARDS)
        pl.semaphore_signal(barrier, inc=1, device_id=(z, peer), device_id_type=MESH)
        return carry

    lax.fori_loop(1, SHARDS, greet, 0)

    loads = []
    for number, (source, target) in enumerate(((fresh, fresh_band), (stale, stale_band))):
        for col in range(5):
            start = pl.multiple_of(lax.rem(superblock + col, SUPER) * TILE, TILE)
            load = pltpu.make_async_copy(
                source.at[:, :, pl.ds(start, TILE)],
                target.at[:, :, pl.ds(col * TILE, TILE)],
                load_sem.at[number, col],
            )
            load.start()
            loads.append(load)

    for load in loads:
        load.wait()
    pl.semaphore_wait(barrier, SHARDS + 1)

    def grad_copy(peer):
        row = lax.rem(f + SHARDS - 16 * (lax.rem(peer, 4) // 2), SHARDS)
        return (
            grad.at[peer // 4],
            whole_grad.at[pl.ds(pl.multiple_of(row * ROWS, ROWS), ROWS), :],
        )

    def grad_remote(peer):
        source, target = grad_copy(peer)
        return pltpu.make_async_remote_copy(
            src_ref=source, dst_ref=target, send_sem=grad_send.at[peer], recv_sem=grad_recv,
            device_id=(z, peer), device_id_type=MESH,
        )

    def grad_step(index):
        @pl.when(index < SHARDS)
        def _():
            grad_remote(lax.rem(f + index, SHARDS)).start()

    def each_peer(act):
        lax.fori_loop(1, SHARDS, lambda s, c: (act(lax.rem(f + s, SHARDS)), c)[1], 0)

    def ring_copy(way, index, train):
        turn = lax.rem(index, 3)
        return pltpu.make_async_remote_copy(
            src_ref=sending.at[(way * 3 + turn) * TRAINS + train],
            dst_ref=log.at[way * STEPS + index * TRAINS + train],
            send_sem=ring_send.at[way, turn, train],
            recv_sem=ring_recv.at[way, index, train],
            device_id=(onward[way], f),
            device_id_type=MESH,
        )

    def hop(index, first):
        for train in range(TRAINS):
            for way in range(2):
                place = index * TRAINS + train
                choice = table[way * STEPS + place]
                own = fresh_band[jnp.maximum(choice, 0)]
                turn = lax.rem(index, 3)
                if not first:
                    ring_copy(way, index - 1, train).wait_recv()

                    @pl.when(index >= 3)
                    def _():
                        ring_copy(way, index - 3, train).wait_send()

                    own = jnp.where(choice < 0, log[way * STEPS + place - TRAINS], own)
                sending[(way * 3 + turn) * TRAINS + train] = own
                ring_copy(way, index, train).start()

    hop(0, True)
    own_grad = pltpu.make_async_copy(*grad_copy(f), grad_recv)
    own_grad.start()

    def hop_and_grads(index, carry):
        hop(index, False)
        for extra in range(GRADS_A_HOP):
            grad_step((index - 1) * GRADS_A_HOP + 1 + extra)
        return carry

    lax.fori_loop(1, hops, hop_and_grads, 0)

    for way in range(2):
        for train in range(TRAINS):
            ring_copy(way, hops - 1, train).wait_recv()
            for turn in range(3):
                ring_copy(way, hops - 3 + turn, train).wait_send()

    def choose(root):
        code = table[CODE_ROW + root]
        used = jnp.maximum(code, 0)
        owner = used // 32
        slot = lax.rem(used, 32)
        away = lax.rem(z - owner + GROUPS, GROUPS)
        ahead = jnp.logical_or(away < REACH, jnp.logical_and(away == REACH, lax.rem(owner, 2) == 0))
        dist = jnp.where(ahead, away, GROUPS - away)
        way = jnp.where(ahead, 0, 1)
        found = table[DIST_ROWS + way * REACH + jnp.maximum(dist - 1, 0)]
        moved = log[way * STEPS + found]
        own = jnp.where(away == 0, fresh_band[slot], moved)
        current[root] = jnp.where(code < 0, stale_band[root], own)

    own_rows = pl.ds(pl.multiple_of(place * ROWS, ROWS), ROWS)
    own_band = pl.ds(pl.multiple_of((place // 4) * TILE, TILE), BAND)

    def deliver(source, target, peer, send_sem, recv_sem, wait):
        @pl.when(peer != f)
        def _():
            copy = pltpu.make_async_remote_copy(
                src_ref=source, dst_ref=target, send_sem=send_sem, recv_sem=recv_sem,
                device_id=(z, peer), device_id_type=MESH,
            )
            if wait:
                copy.wait_send()
            else:
                copy.start()

        if not wait:

            @pl.when(peer == f)
            def _():
                pltpu.make_async_copy(source, target, recv_sem).start()

    def left_send_step(step, wait):
        turn = lax.rem(f + step, 16)
        number = turn // 2
        half = lax.rem(turn, 2)
        peer = 4 * number + 2 * half + place // 8
        root = current.at[2 * number]

        @pl.when(half == own_half)
        def _():
            deliver(root, left_in.at[own_rows, own_band], peer, left_send.at[turn], left_recv.at[0], wait)

        @pl.when(half != own_half)
        def _():
            deliver(
                root.at[:, pl.ds(TILE, REST)], left_out.at[own_rows, :], peer,
                left_send.at[turn], left_recv.at[1], wait,
            )

    def right_send_step(step, wait):
        turn = lax.rem(f + step, 16)
        number = turn // 2
        peer = 4 * number + 2 * lax.rem(turn, 2) + own_half
        root = current.at[2 * number + 1]
        deliver(root, right_in.at[own_rows, own_band], peer, right_send.at[turn], right_recv, wait)

    def repeat(count, act):
        lax.fori_loop(0, count, lambda i, c: (act(i), c)[1], 0)

    for root in range(0, ROOTS, 2):
        choose(root)
    repeat(16, lambda step: left_send_step(step, False))
    for root in range(1, ROOTS, 2):
        choose(root)
    repeat(16, lambda step: right_send_step(step, False))

    sibling = f + 1 - 2 * col_half

    def hand(source, target, send_sem, recv_sem):
        return pltpu.make_async_remote_copy(
            src_ref=source, dst_ref=target, send_sem=send_sem, recv_sem=recv_sem,
            device_id=(z, sibling), device_id_type=MESH,
        )

    def await_bytes(window, sem):
        pltpu.make_async_copy(window, window, sem).wait()

    pltpu.make_async_copy(whole_grad, whole_grad, grad_recv).wait()

    def add_squares(index, total):
        rows = whole_grad[pl.ds(pl.multiple_of(index * 32, 32), 32), :].astype(jnp.float32)
        squares = (rows * rows).reshape(4, 8, 8, TILE)
        return total + jnp.sum(squares, axis=(0, 2))

    grad_square = lax.fori_loop(0, WIDTH // 32, add_squares, jnp.zeros((8, TILE), jnp.float32))

    await_bytes(left_in.at[pl.ds(0, 256), pl.ds(0, BAND)], left_recv.at[0])
    await_bytes(left_out.at[pl.ds(0, 256), :], left_recv.at[1])
    hands = []
    for index in range(2):
        start = pl.multiple_of((2 * col_half + index) * TILE, TILE)
        window = left_in.at[pl.ds(start, TILE), pl.ds(start, BAND)]
        hands.append(hand(window, window, left_pass.at[index], left_passed))
    window = left_out.at[pl.ds(pl.multiple_of(256 * col_half, 256), 256), :]
    hands.append(hand(window, window, left_pass.at[2], left_passed))
    for copy in hands:
        copy.start()
    def left_step(index):
        cols = pl.ds(pl.multiple_of(index * 256, 256), 256)
        left_product[:, cols] = jnp.dot(
            left_in[...], whole_grad[:, cols], preferred_element_type=jnp.float32
        ).astype(jnp.bfloat16)

    await_bytes(right_in.at[:, pl.ds(0, BAND)], right_recv)
    for index in range(4):
        rows = pl.ds(index * TILE, TILE)
        source = right_in.at[rows, pl.ds((index + 1) * TILE, REST)]
        copy = hand(source, right_out.at[rows, :], right_pass.at[index], right_passed)
        copy.start()
        hands.append(copy)
    await_bytes(left_in.at[pl.ds(0, 256), :], left_passed)

    fill_near(left_in)
    fill_far(left_in, left_out)
    repeat(4, left_step)
    fill_near(right_in)
    near_cols = pl.ds(pl.multiple_of(col_half * HALF, HALF), HALF)
    next_cols = pl.ds(pl.multiple_of((1 - col_half) * HALF, HALF), TILE)
    last_cols = pl.ds(pl.multiple_of((1 - col_half) * HALF + TILE, TILE), REST)

    def times(rows, cols, start, size):
        return lax.dot_general(
            left_product[rows, cols], right_in[:, start : start + size], (((1,), (1,)), ((), ())),
            preferred_element_type=jnp.float32,
        )

    def near_step(index):
        rows = pl.ds(pl.multiple_of(index * TILE, TILE), TILE)
        product[rows, :] = times(rows, near_cols, 0, HALF) + times(rows, next_cols, HALF, TILE)

    repeat(4, near_step)
    await_bytes(right_out, right_passed)
    fill_far(right_in, right_out)

    def tile_step(row, wait):
        deliver(
            tile.at[pl.ds(pl.multiple_of(row * ROWS, ROWS), ROWS), :],
            tiles.at[block, :, near_cols],
            row_half * 16 + row, tile_send.at[row], tile_recv, wait,
        )

    def last_step(index, total):
        rows = pl.ds(pl.multiple_of(index * TILE, TILE), TILE)
        value = product[rows, :] + times(rows, last_cols, BAND, REST)
        tile[rows, :] = value.astype(jnp.bfloat16)
        squares = (value * value).reshape(16, 8, 4, TILE)
        return total + jnp.sum(squares, axis=(0, 2))

    update_part = lax.fori_loop(0, 4, last_step, jnp.zeros((8, TILE), jnp.float32))
    update_part = jnp.sum(update_part, axis=0, keepdims=True)
    grad_part = jnp.sum(grad_square, axis=0, keepdims=True)
    line = lax.broadcasted_iota(jnp.int32, (8, TILE), 0)
    sums_out[...] = jnp.where(line == 0, update_part, grad_part)

    def sum_step(step, wait):
        peer = 4 * block + lax.rem(part + step, 4)
        deliver(sums_out, sums.at[part], peer, sum_send.at[step], sum_recv, wait)

    def total_step(step, wait):
        peer = row_half * 16 + 2 * lax.rem(step + block, 8) + col_half
        deliver(totals_out, totals.at[block], peer, total_send.at[step], total_recv, wait)

    repeat(4, lambda step: sum_step(step, False))
    repeat(16, lambda step: tile_step(lax.rem(step + 4 * block, 16), False))
    await_bytes(sums, sum_recv)
    update_part = (sums[0] + sums[1]) + (sums[2] + sums[3])
    totals_out[...] = jnp.where(line == 0, update_part, grad_part)
    repeat(8, lambda step: total_step(step, False))

    each_peer(lambda peer: grad_remote(peer).wait_send())
    repeat(16, lambda step: left_send_step(step, True))
    repeat(16, lambda step: right_send_step(step, True))
    for copy in hands:
        copy.wait_send()
    await_bytes(totals, total_recv)
    ratios = []
    for number in range(BLOCKS):
        update_square = jnp.sum(totals[number, 0:1, :], axis=1, keepdims=True)
        grad_total = jnp.sum(totals[number, 1:2, :], axis=1, keepdims=True)
        ratios.append(jnp.sqrt(grad_total) * lax.rsqrt(update_square + epsilon))
    await_bytes(tiles, tile_recv)
    for number in range(BLOCKS):
        out[number] = (ratios[number] * tiles[number].astype(jnp.float32)).astype(jnp.bfloat16)
    repeat(16, lambda row: tile_step(row, True))
    repeat(4, lambda step: sum_step(step, True))
    repeat(8, lambda step: total_step(step, True))


def ring_exchange(hops, table, grad_blocks, stale_roots, fresh_roots):
    bf16, f32 = jnp.bfloat16, jnp.float32
    dma = pltpu.SemaphoreType.DMA
    vmem = pltpu.VMEM
    smem_spec = pl.BlockSpec(memory_space=pltpu.SMEM)
    any_spec = pl.BlockSpec(memory_space=pl.ANY)
    vmem_spec = pl.BlockSpec(memory_space=pltpu.VMEM)
    return pl.pallas_call(
        functools.partial(main_kernel, hops),
        out_shape=jax.ShapeDtypeStruct((BLOCKS, ROWS, WIDTH), bf16),
        in_specs=[smem_spec, any_spec, any_spec, any_spec],
        out_specs=vmem_spec,
        scratch_shapes=[
            vmem((ROOTS, ROWS, BAND), bf16),
            vmem((ROOTS, ROWS, BAND), bf16),
            vmem((ROOTS, ROWS, BAND), bf16),
            vmem((6 * TRAINS, ROWS, BAND), bf16),
            vmem((2 * STEPS, ROWS, BAND), bf16),
            vmem((WIDTH, WIDTH), bf16),
            vmem((HALF, WIDTH), bf16),
            vmem((HALF, REST), bf16),
            vmem((HALF, WIDTH), bf16),
            vmem((HALF, REST), bf16),
            vmem((HALF, WIDTH), bf16),
            vmem((HALF, HALF), f32),
            vmem((HALF, HALF), bf16),
            vmem((BLOCKS, ROWS, WIDTH), bf16),
            vmem((4, 8, TILE), f32),
            vmem((8, TILE), f32),
            vmem((BLOCKS, 8, TILE), f32),
            vmem((8, TILE), f32),
            dma((2, 5)),
            dma((2, 3, TRAINS)),
            dma((2, hops, TRAINS)),
            dma((SHARDS,)),
            dma(()),
            dma((16,)),
            dma((2,)),
            dma((3,)),
            dma(()),
            dma((16,)),
            dma(()),
            dma((4,)),
            dma(()),
            dma((4,)),
            dma(()),
            dma((8,)),
            dma(()),
            dma((16,)),
            dma(()),
        ],
        compiler_params=pltpu.CompilerParams(
            collective_id=HOPS.index(hops), has_side_effects=True, vmem_limit_bytes=48 << 20
        ),
    )(table, grad_blocks, stale_roots, fresh_roots)


def local(grad_blocks, stale_roots, fresh_roots, owner_list, slot_list, refresh_flags):
    table = schedule(owner_list, slot_list, refresh_flags)

    def by_ring(hops):
        return lambda _: ring_exchange(hops, table, grad_blocks, stale_roots, fresh_roots)

    def by_all(_):
        return whole_exchange(
            grad_blocks, stale_roots, fresh_roots, owner_list, slot_list, refresh_flags
        )

    need = table[NEED_ROW]
    path = sum((need > hops).astype(jnp.int32) for hops in HOPS)
    return lax.switch(path, [by_ring(hops) for hops in HOPS] + [by_all], None)


def solution(mesh):
    placed = (
        P("group", "fsdp", None),
        P("group", "fsdp", None),
        P("group", "fsdp", None),
        P(),
        P(),
        P(),
    )
    return jax.shard_map(
        local, mesh=mesh, in_specs=placed, out_specs=P("group", "fsdp", None), check_vma=False
    )
```
